32 devices in a mesh: win: 2 (over y), pair: 4 (over z), stk: 2 (over x), lag: 2 (over core).
Axes of the slice: x: 2, y: 2, z: 4, core: 2. Of those that a mesh axis runs over, the one named last changes fastest.
Arguments:
- spectra: bfloat16 [32, 4, 256, 1024], P('win', 'pair', 'stk'), parts along dimension 0, may hold values from -40 to 40
- pair_blocks: int32 [8, 40, 2], P('win'), parts along dimension 0, may hold values from 0 to 63, as said below
- live_pairs: int32 [8], P('win'), parts along dimension 0, may hold values from 10 to 40, as said below
- stack_group: int32 [8, 40], P('win'), parts along dimension 0, may hold values from 0 to 3, as said below
Outputs:
- stacks: float32 [8, 256, 1024], P('win', 'stk', ('pair', 'lag')), parts along dimension 0
The draws below stay inside these ranges and needn't reach their ends.
There are 2 independent parts, one for each index of `win`. The reference program is written for one: setup_inputs(seed, part) draws one part's arguments, and reference() takes and returns one part's arrays. A program takes and returns all parts, laid end to end along the dimension named above; each array names one. Nothing has to cross between parts.
Inputs may be any that keep to these rules, and one draw needn't show every extreme that they name: `pair_blocks`: every pair names a first block and a second block 1 to 8 higher. The pairs of all 40 slots of one owner span exactly 32 consecutive blocks, from the smallest first block to the largest second block. An owner's first live_pairs slots are used, the rest are not. Some owner uses all 40. `stack_group`: in the first 4 slots of every owner each group stands once.
All inputs are finite; a program needn't handle non-finite values.
Results may differ from the reference program's by a relative error of at most 0.0058.
Values may be sent and summed in bfloat16 or wider, within the bound.
No kernel may reach another device: no remote copies, remote signals or barrier semaphores. Data moves between devices by JAX's collectives and lax.ppermute only.
A program may use at most 128 MiB of HBM per device.

```python
import math
import jax
import jax.numpy as jnp
from jax import lax

FREQ = 512
CH_BLK = 256
NBLK = 64
WINB = 32
MAXOFF = 8
PB_DEV = 40
NGRP = 4
HW = 15
BLK_DEV = 16
N_PAIR = 4


def draw_spectra(key, part):
    shape_full = (BLK_DEV, N_PAIR, CH_BLK, 2 * FREQ)
    scale_key, noise_key = jax.random.split(key, 2)
    channel_scale = jnp.exp(jax.random.uniform(scale_key, (BLK_DEV, N_PAIR, CH_BLK, 1), jnp.float32, 0.0, math.log(10.0)))
    values = channel_scale * jax.random.truncated_normal(noise_key, -4.0, 4.0, shape_full, jnp.float32)
    return values.astype(jnp.bfloat16)


def owner_plan(key):
    plan_key = jax.random.fold_in(key, 4242)
    start_key, pick_key, live_key, full_key, group_key, cycle_key = jax.random.split(plan_key, 6)
    edge_key = jax.random.fold_in(plan_key, 77)
    low_key, step_key = jax.random.split(edge_key)
    choices_total = (WINB - MAXOFF) * MAXOFF
    starts = jax.random.randint(start_key, (N_PAIR,), 0, NBLK - WINB + 1)
    low_owner = jax.random.randint(low_key, (), 0, N_PAIR)
    high_owner = (low_owner + jax.random.randint(step_key, (), 1, N_PAIR)) % N_PAIR
    owner_ids = jnp.arange(N_PAIR)
    starts = jnp.where(owner_ids == low_owner, 0, starts)
    starts = jnp.where(owner_ids == high_owner, NBLK - WINB, starts)

    def pick_slots(owner_key):
        middle_key, order_key = jax.random.split(owner_key)
        middle = jax.random.permutation(middle_key, choices_total - 2) + 1
        chosen = jnp.concatenate([jnp.array([0, choices_total - 1], jnp.int32), middle[:PB_DEV - 2].astype(jnp.int32)])
        return jax.random.permutation(order_key, chosen)
    picked = jax.vmap(pick_slots)(jax.random.split(pick_key, N_PAIR))
    first_block = starts[:, None] + picked // MAXOFF
    second_block = first_block + picked % MAXOFF + 1
    pair_blocks = jnp.stack([first_block, second_block], axis=-1).astype(jnp.int32)
    halving = jax.random.randint(live_key, (N_PAIR,), 0, 4)
    live_counts = jnp.maximum(PB_DEV // 4, PB_DEV // jnp.left_shift(1, halving))
    busiest = jax.random.randint(full_key, (), 0, N_PAIR)
    live_counts = jnp.where(jnp.arange(N_PAIR) == busiest, PB_DEV, live_counts).astype(jnp.int32)
    groups = jax.random.randint(group_key, (N_PAIR, PB_DEV), 0, NGRP)
    cycle_shift = jax.random.randint(cycle_key, (N_PAIR, 1), 0, NGRP)
    slot_ids = jnp.arange(PB_DEV)[None, :]
    groups = jnp.where(slot_ids < NGRP, (slot_ids + cycle_shift) % NGRP, groups).astype(jnp.int32)
    return (pair_blocks, live_counts, groups)


def draw_pair_blocks(key, part):
    return owner_plan(key)[0]


def draw_live_pairs(key, part):
    return owner_plan(key)[1]


def draw_stack_group(key, part):
    return owner_plan(key)[2]


def setup_inputs(seed: int = 0, part: int = 0) -> dict:
    seeds = jax.random.split(jax.random.key(seed), 5)
    own_keys = jax.random.split(jax.random.fold_in(seeds[4], part), 5)
    return {
        "spectra": draw_spectra(jax.random.fold_in(jax.random.fold_in(seeds[4], part), 71), part),
        "pair_blocks": draw_pair_blocks(jax.random.fold_in(jax.random.fold_in(seeds[4], part), 71), part),
        "live_pairs": draw_live_pairs(jax.random.fold_in(jax.random.fold_in(seeds[4], part), 71), part),
        "stack_group": draw_stack_group(jax.random.fold_in(jax.random.fold_in(seeds[4], part), 71), part),
    }


AMP_FLOOR = 0.5
EPSILON = 1e-06

def lag_table(lag_ids, num_bins):
    bin_index = jnp.arange(num_bins, dtype=jnp.int32)[:, None]
    phase_turns = bin_index * (lag_ids[None, :] + num_bins) % (2 * num_bins)
    angles = phase_turns.astype(jnp.float32) * (math.pi / num_bins)
    cosine = jnp.cos(angles)
    sine_part = jnp.sin(angles)
    amp_scale = math.sqrt(2.0 / num_bins)
    upper_rows = jnp.concatenate([cosine, sine_part], axis=1)
    lower_rows = jnp.concatenate([-sine_part, cosine], axis=1)
    return (jnp.concatenate([upper_rows, lower_rows], axis=0) * amp_scale).astype(jnp.bfloat16)

def whiten_blocks(spectra):
    values = spectra.astype(jnp.float32)
    channel_power = lax.optimization_barrier(jnp.mean(values * values, axis=-1, keepdims=True)) * 2.0
    return (values / jnp.sqrt(channel_power + EPSILON)).astype(jnp.bfloat16)

def cross_spectra(first_spec, second_spec, num_bins):
    first_spec = first_spec.astype(jnp.float32)
    second_spec = second_spec.astype(jnp.float32)
    real_a = first_spec[..., :num_bins]
    imag_a = first_spec[..., num_bins:]
    real_b = second_spec[..., :num_bins]
    imag_b = second_spec[..., num_bins:]
    real_part = real_a * real_b + imag_a * imag_b
    imag_part = imag_a * real_b - real_a * imag_b
    return jnp.concatenate([real_part, imag_part], axis=-1).astype(jnp.bfloat16)

def phase_terms(correlation, half_lags):
    direct = correlation[:, :half_lags]
    quadrature = correlation[:, half_lags:]
    divisor = jnp.maximum(jnp.sqrt(direct * direct + quadrature * quadrature), AMP_FLOOR)
    return jnp.stack([direct, direct / divisor, quadrature / divisor], axis=1)

def reference(spectra, pair_blocks, live_pairs, stack_group):
    num_bins = FREQ
    channels = CH_BLK
    lag_count = 2 * num_bins
    whitened = whiten_blocks(spectra).reshape(NBLK, channels, 2 * num_bins)
    table_all = lag_table(jnp.arange(lag_count, dtype=jnp.int32), num_bins)
    slot_index = jnp.arange(PB_DEV, dtype=jnp.int32)
    group_index = jnp.arange(NGRP, dtype=jnp.int32)

    def owner_step(group_sums, inputs):
        owner_pairs, owner_live, owner_groups = inputs
        first_spec = jnp.take(whitened, owner_pairs[:, 0].astype(jnp.int32), axis=0)
        second_spec = jnp.take(whitened, owner_pairs[:, 1].astype(jnp.int32), axis=0)
        cross_rows = cross_spectra(first_spec, second_spec, num_bins).reshape(PB_DEV * channels, 2 * num_bins)
        correlation = jnp.dot(cross_rows, table_all, preferred_element_type=jnp.float32)
        phase_rows = phase_terms(correlation, lag_count).reshape(PB_DEV, channels * 3 * lag_count)
        weights = ((owner_groups[:, None] == group_index[None, :]) & (slot_index < owner_live)[:, None]).astype(jnp.float32)
        return (group_sums + jnp.dot(weights.T, phase_rows, precision=lax.Precision.HIGHEST), None)
    initial = jnp.zeros((NGRP, channels * 3 * lag_count), jnp.float32)
    group_sums, unused = lax.scan(owner_step, initial, (pair_blocks, live_pairs, stack_group))
    group_sums = group_sums.reshape(NGRP, channels, 3, lag_count)
    live_mask = slot_index[None, :] < live_pairs[:, None]
    member = (stack_group[:, :, None] == group_index[None, None, :]) & live_mask[:, :, None]
    members = lax.optimization_barrier(jnp.sum(member.astype(jnp.float32), axis=(0, 1)))
    norm_root = jnp.sqrt(members)[:, None, None]
    linear = group_sums[:, :, 0] / norm_root
    coherence = jnp.sqrt(group_sums[:, :, 1] * group_sums[:, :, 1] + group_sums[:, :, 2] * group_sums[:, :, 2]) / norm_root
    padded = jnp.pad(coherence, ((0, 0), (0, 0), (HW, HW)))
    smoothed = jnp.zeros_like(coherence)
    for offset_tap in range(2 * HW + 1):
        smoothed = smoothed + padded[:, :, offset_tap:offset_tap + lag_count]
    smoothed = smoothed / (2 * HW + 1)
    return linear * smoothed * smoothed
```

```python
import functools
import math

import jax
import jax.numpy as jnp
from jax import lax
from jax.experimental import pallas as pl
from jax.experimental.pallas import tpu as pltpu
from jax.sharding import PartitionSpec as P

NGRP = 4
HW = 15

AMP_FLOOR = 0.5
EPSILON = 1e-06
TILE_ROWS = 256
UNIT_ROWS = 16
LAG_TILE = 256
CHUNKS = 4


def lag_table(lag_count, num_bins):
    lag_ids = jnp.arange(lag_count, dtype=jnp.int32)
    bin_index = jnp.arange(num_bins, dtype=jnp.int32)[:, None]
    phase_turns = bin_index * (lag_ids[None, :] + num_bins) % (2 * num_bins)
    angles = phase_turns.astype(jnp.float32) * (math.pi / num_bins)
    cosine = jnp.cos(angles)
    sine_part = jnp.sin(angles)
    amp_scale = math.sqrt(2.0 / num_bins)
    upper_rows = jnp.concatenate([cosine, sine_part], axis=1)
    lower_rows = jnp.concatenate([-sine_part, cosine], axis=1)
    return (jnp.concatenate([upper_rows, lower_rows], axis=0) * amp_scale).astype(jnp.bfloat16)


def window_sum(values):
    rows, lags = values.shape
    edge = jnp.zeros((rows, 128), jnp.float32)
    one = jnp.concatenate([edge, values, edge], axis=1)
    width = one.shape[1]
    two = one + pltpu.roll(one, 1, 1)
    four = two + pltpu.roll(two, 2, 1)
    eight = four + pltpu.roll(four, 4, 1)
    back = eight + pltpu.roll(eight, 8, 1)
    ahead = eight + pltpu.roll(four, 8, 1) + pltpu.roll(two, 12, 1) + pltpu.roll(one, 14, 1)
    return (back + pltpu.roll(ahead, width - HW, 1))[:, 128 : 128 + lags]


def stack_kernel(num_parts, cell, tiles_ref, groups_ref, norm_ref, *refs):
    part_refs = refs[:num_parts]
    first_ref, second_ref, table_ref, out_ref, white_ref, sums_ref = refs[num_parts:]
    part_rows, width = part_refs[0].shape
    num_bins = width // 2
    lag_count = table_ref.shape[1] // 2
    units = TILE_ROWS // UNIT_ROWS

    for part, ref in enumerate(part_refs):
        values = ref[...].astype(jnp.float32)
        power = jnp.sum(values * values, axis=1, keepdims=True) * (2.0 / width)
        white = values * lax.rsqrt(power + EPSILON)
        white_ref[part * part_rows : (part + 1) * part_rows, :] = white.astype(jnp.bfloat16)
    sums_ref[...] = jnp.zeros_like(sums_ref)

    def tile_step(tile, carry):
        rows = pl.ds(pl.multiple_of(tile * TILE_ROWS, TILE_ROWS), TILE_ROWS)
        white = white_ref[...]
        first = jnp.dot(first_ref[rows, :], white, preferred_element_type=jnp.float32)
        second = jnp.dot(second_ref[rows, :], white, preferred_element_type=jnp.float32)
        real_a, imag_a = first[:, :num_bins], first[:, num_bins:]
        real_b, imag_b = second[:, :num_bins], second[:, num_bins:]
        real_part = (real_a * real_b + imag_a * imag_b).astype(jnp.bfloat16)
        imag_part = (imag_a * real_b - real_a * imag_b).astype(jnp.bfloat16)
        cross = jnp.concatenate([real_part, imag_part], axis=1)
        for lag in range(0, lag_count, LAG_TILE):
            lags = slice(lag, lag + LAG_TILE)
            quad_lags = slice(lag_count + lag, lag_count + lag + LAG_TILE)
            direct = jnp.dot(cross, table_ref[:, lags], preferred_element_type=jnp.float32)
            quad = jnp.dot(cross, table_ref[:, quad_lags], preferred_element_type=jnp.float32)
            inverse = jnp.minimum(lax.rsqrt(direct * direct + quad * quad), 1.0 / AMP_FLOOR)
            phase_c = direct * inverse
            phase_s = quad * inverse
            for unit in range(units):
                group = groups_ref[tile * units + unit]
                own = slice(unit * UNIT_ROWS, (unit + 1) * UNIT_ROWS)
                sums_ref[0, group, :, lags] += direct[own]
                sums_ref[1, group, :, lags] += phase_c[own]
                sums_ref[2, group, :, lags] += phase_s[own]
        return carry

    lax.fori_loop(0, tiles_ref[0], tile_step, 0)

    linear, coherence = [], []
    for group in range(NGRP):
        folded = []
        for kind in range(3):
            whole = sums_ref[kind, group]
            total = whole[:cell]
            for start in range(cell, UNIT_ROWS, cell):
                total = total + whole[start : start + cell]
            folded.append(total)
        scale = norm_ref[group]
        linear.append(folded[0] * scale)
        coherence.append(jnp.sqrt(folded[1] * folded[1] + folded[2] * folded[2]) * scale)
    coherence = jnp.concatenate(coherence, axis=0)
    smoothed = window_sum(coherence) * (1.0 / (2 * HW + 1))
    for group in range(NGRP):
        own = smoothed[group * cell : (group + 1) * cell]
        out_ref[group] = linear[group] * own * own


def pair_order(pair_blocks, live_pairs, stack_group, parts, part_blocks, cell):
    owners, slots, _ = pair_blocks.shape
    total = owners * slots
    unit_pairs = UNIT_ROWS // cell
    tile_pairs = TILE_ROWS // cell
    places = -(-(total + NGRP * (unit_pairs - 1)) // tile_pairs) * tile_pairs
    group_index = jnp.arange(NGRP, dtype=jnp.int32)
    live = jnp.arange(slots, dtype=jnp.int32)[None, :] < live_pairs[:, None]
    member = (stack_group[:, :, None] == group_index) & live[:, :, None]
    member = member.reshape(total, NGRP).astype(jnp.int32)
    members = jnp.sum(member, axis=0)
    filled = (members + unit_pairs - 1) // unit_pairs * unit_pairs
    ends = jnp.cumsum(filled)
    rank = jnp.cumsum(member, axis=0) - 1
    place = jnp.sum(member * (rank + (ends - filled)[None, :] + 1), axis=1) - 1
    here = jnp.arange(places, dtype=jnp.int32)
    match = here[:, None] == place[None, :]
    me = lax.axis_index("pair")
    blocks = pair_blocks.reshape(total, 2)
    held = lax.rem(me - lax.rem(blocks, parts) + parts, parts) * part_blocks + blocks // parts
    taken = jnp.sum(jnp.where(match[:, :, None], held[None] + 1, 0), axis=1) - 1
    row = jnp.where(taken[:, None, :] < 0, -1, taken[:, None, :] * cell + jnp.arange(cell, dtype=jnp.int32)[None, :, None])
    row = row.reshape(places * cell, 2)
    column = jnp.arange(parts * part_blocks * cell, dtype=jnp.int32)[None, :]
    first = (row[:, :1] == column).astype(jnp.bfloat16)
    second = (row[:, 1:] == column).astype(jnp.bfloat16)
    unit_start = jnp.arange(places // unit_pairs, dtype=jnp.int32) * unit_pairs
    unit_group = jnp.minimum(jnp.sum((unit_start[:, None] >= ends[None, :]).astype(jnp.int32), axis=1), NGRP - 1)
    tiles = ((ends[-1] + tile_pairs - 1) // tile_pairs).reshape(1)
    norm = 1.0 / jnp.sqrt(members.astype(jnp.float32))
    return tiles, unit_group, norm, first, second


def shards(spectra, pair_blocks, live_pairs, stack_group):
    parts = lax.axis_size("pair")
    me = lax.axis_index("pair")
    cores = lax.axis_size("lag")
    core = lax.axis_index("lag")
    part_blocks, _, channels, width = spectra.shape
    num_bins = width // 2
    lag_count = 2 * num_bins
    own_channels = channels // (parts * cores)
    chunks = CHUNKS if own_channels % CHUNKS == 0 else 1
    cell = own_channels // chunks

    tiles, unit_group, norm, first, second = pair_order(
        pair_blocks, live_pairs, stack_group, parts, part_blocks, cell
    )
    table = lag_table(lag_count, num_bins)

    rows = part_blocks * cell
    inputs = 1 if rows % UNIT_ROWS else parts
    call = pl.pallas_call(
        functools.partial(stack_kernel, inputs, cell),
        out_shape=jax.ShapeDtypeStruct((NGRP, cell, lag_count), jnp.float32),
        in_specs=[pl.BlockSpec(memory_space=pltpu.SMEM)] * 3
        + [pl.BlockSpec(memory_space=pltpu.VMEM)] * (inputs + 3),
        out_specs=pl.BlockSpec(memory_space=pltpu.VMEM),
        scratch_shapes=[
            pltpu.VMEM((parts * rows, width), jnp.bfloat16),
            pltpu.VMEM((3, NGRP, UNIT_ROWS, lag_count), jnp.float32),
        ],
        compiler_params=pltpu.CompilerParams(vmem_limit_bytes=40 * 1024 * 1024),
        name="stack",
    )

    stacks = []
    for chunk in range(chunks):
        received = []
        for shift in range(parts):
            target = lax.rem(me + shift, parts)
            start = (target * cores + core) * own_channels + chunk * cell
            piece = lax.dynamic_slice_in_dim(spectra, start, cell, 2).reshape(rows, width)
            if shift:
                piece = lax.ppermute(piece, "pair", [(i, (i + shift) % parts) for i in range(parts)])
            received.append(piece)
        if rows % UNIT_ROWS:
            received = [jnp.concatenate(received, axis=0)]
        stacks.append(call(tiles, unit_group, norm, *received, first, second, table))
    stacks = jnp.concatenate(stacks, axis=1)
    return lax.all_to_all(stacks, ("pair", "lag"), 2, 1, tiled=True)


def solution(mesh):
    return jax.shard_map(
        shards,
        mesh=mesh,
        in_specs=(P("win", "pair", "stk", None), P("win", None, None), P("win"), P("win", None)),
        out_specs=P("win", "stk", ("pair", "lag")),
        check_vma=False,
    )
```

```python
import functools
import math

import jax
import jax.numpy as jnp
from jax import lax
from jax.experimental import pallas as pl
from jax.experimental.pallas import tpu as pltpu
from jax.sharding import PartitionSpec as P

NGRP = 4
HW = 15

AMP_FLOOR = 0.5
EPSILON = 1e-06
TILE_ROWS = 256
PACK_ROWS = 16
SUB_ROWS = 8
LANES = 128
CLASSES = 4


def turn(steps, period):
    quarter = period // 4
    quadrant = (steps + quarter // 2) // quarter
    angle = (steps - quadrant * quarter).astype(jnp.float32) * (2.0 * math.pi / period)
    square = angle * angle
    cosine = 1.0 + square * (-1 / 2 + square * (1 / 24 + square * (-1 / 720 + square * (1 / 40320))))
    sine = angle * (1.0 + square * (-1 / 6 + square * (1 / 120 + square * (-1 / 5040 + square * (1 / 362880)))))
    odd = (quadrant & 1) == 1
    cosine, sine = jnp.where(odd, sine, cosine), jnp.where(odd, cosine, sine)
    cosine = jnp.where(((quadrant + 1) & 2) == 2, -cosine, cosine)
    sine = jnp.where((quadrant & 2) == 2, -sine, sine)
    return cosine, sine


def table_kernel(used_ref, out_ref):
    width, columns = out_ref.shape
    num_bins = width // 2
    period = 2 * num_bins
    scale = math.sqrt(2.0 / num_bins)
    class_bins = num_bins // CLASSES
    rows = lax.broadcasted_iota(jnp.int32, (class_bins, LANES), 0)
    lanes = lax.broadcasted_iota(jnp.int32, (class_bins, LANES), 1)
    for index in range(CLASSES):
        real_rows = slice(2 * index * class_bins, (2 * index + 1) * class_bins)
        imag_rows = slice((2 * index + 1) * class_bins, (2 * index + 2) * class_bins)
        for tile in range(columns // (2 * LANES)):
            lags = lanes + (tile * LANES + num_bins)
            cosine, sine = turn((rows * CLASSES + index) * lags & (period - 1), period)
            cosine, sine = cosine * scale, sine * scale
            direct = slice(2 * tile * LANES, (2 * tile + 1) * LANES)
            quad = slice((2 * tile + 1) * LANES, (2 * tile + 2) * LANES)
            out_ref[real_rows, direct] = cosine.astype(jnp.bfloat16)
            out_ref[imag_rows, direct] = (-sine).astype(jnp.bfloat16)
            out_ref[real_rows, quad] = sine.astype(jnp.bfloat16)
            out_ref[imag_rows, quad] = cosine.astype(jnp.bfloat16)


def lag_table(used, lag_count, num_bins):
    return pl.pallas_call(
        table_kernel,
        out_shape=jax.ShapeDtypeStruct((2 * num_bins, 2 * lag_count // CLASSES), jnp.bfloat16),
        in_specs=[pl.BlockSpec(memory_space=pltpu.SMEM)],
        out_specs=pl.BlockSpec(memory_space=pltpu.VMEM),
        compiler_params=pltpu.CompilerParams(vmem_limit_bytes=6 * 1024 * 1024),
        name="table",
    )(used)


def whiten(values):
    values = values.astype(jnp.float32)
    power = jnp.sum(values * values, axis=-1, keepdims=True) * (2.0 / values.shape[-1])
    return (values * lax.rsqrt(power + EPSILON)).astype(jnp.bfloat16)


def prepare_kernel(chunks, start_ref, spectra_ref, *refs):
    parts = start_ref.shape[0]
    out_refs = refs[: parts * len(chunks)]
    raw_ref, arrived = refs[parts * len(chunks) :]
    _, blocks, own_channels, width = raw_ref.shape
    num_bins = width // 2
    class_bins = num_bins // CLASSES
    order = (2, 3, 1, 0) if parts == 4 else tuple(range(parts))

    def fetch(step):
        start = pl.multiple_of(start_ref[step], 2 * SUB_ROWS)
        return pltpu.make_async_copy(
            spectra_ref.at[:, 0, pl.ds(start, own_channels), :], raw_ref.at[step], arrived.at[step]
        )

    for step in order:
        fetch(step).start()
    source = lax.broadcasted_iota(jnp.int32, (num_bins, num_bins), 0)
    target = lax.broadcasted_iota(jnp.int32, (num_bins, num_bins), 1)
    wanted = (target & (class_bins - 1)) * CLASSES + target // class_bins
    shuffle = jnp.where(source == wanted, 1.0, 0.0).astype(jnp.bfloat16)
    for step in order:
        fetch(step).wait()
        white = whiten(raw_ref[step].reshape(blocks * own_channels, width))
        halves = [
            jnp.dot(white[:, start : start + num_bins], shuffle, preferred_element_type=jnp.float32)
            for start in (0, num_bins)
        ]
        halves = [half.reshape(blocks, own_channels, num_bins) for half in halves]
        offset = 0
        for index, cells in enumerate(chunks):
            out_ref = out_refs[step * len(chunks) + index]
            row = 0
            for cell in cells:
                group = SUB_ROWS // cell
                for block in range(0, blocks, 2 * group):
                    for side, half in enumerate(halves):
                        rows = [half[block + k, offset : offset + cell] for k in range(2 * group)]
                        rows = jnp.concatenate(rows, axis=0).astype(jnp.bfloat16)
                        out_ref[row : row + PACK_ROWS, side * num_bins : (side + 1) * num_bins] = rows
                    row += PACK_ROWS
                offset += cell


def window_sum(values):
    rows, lags = values.shape
    edge = jnp.zeros((rows, 128), jnp.float32)
    one = jnp.concatenate([edge, values, edge], axis=1)
    width = one.shape[1]
    two = one + pltpu.roll(one, 1, 1)
    four = two + pltpu.roll(two, 2, 1)
    eight = four + pltpu.roll(four, 4, 1)
    back = eight + pltpu.roll(eight, 8, 1)
    ahead = eight + pltpu.roll(four, 8, 1) + pltpu.roll(two, 12, 1) + pltpu.roll(one, 14, 1)
    return (back + pltpu.roll(ahead, width - HW, 1))[:, 128 : 128 + lags]


def chunk_rows(cells, unit_pairs):
    return unit_pairs * sum(cells)


def quarter_turns(direct, quad):
    even_d, even_q = direct[0] + direct[2], quad[0] + quad[2]
    odd_d, odd_q = direct[1] + direct[3], quad[1] + quad[3]
    even_e, even_r = direct[0] - direct[2], quad[0] - quad[2]
    odd_e, odd_r = direct[1] - direct[3], quad[1] - quad[3]
    return (
        [even_d + odd_d, even_e - odd_r, even_d - odd_d, even_e + odd_r],
        [even_q + odd_q, even_r + odd_e, even_q - odd_q, even_r - odd_e],
    )


def phase_terms(direct, quad):
    inverse = jnp.minimum(lax.rsqrt(direct * direct + quad * quad), 1.0 / AMP_FLOOR)
    return [direct, direct * inverse, quad * inverse]


def stack_kernel(num_parts, cells, unit_pairs, tile_units, tiles_ref, place_ref, groups_ref, norm_ref, *refs):
    part_refs = refs[:num_parts]
    table_ref, out_ref = refs[num_parts : num_parts + 2]
    white_refs = refs[num_parts + 2 : num_parts + 2 + len(cells)]
    cross_ref, lag_ref, sums_ref = refs[num_parts + 2 + len(cells) :]
    part_rows, width = part_refs[0].shape
    num_bins = width // 2
    class_bins = num_bins // CLASSES
    quarter = width // CLASSES
    unit_rows = chunk_rows(cells, unit_pairs)
    part_blocks = part_rows // sum(cells)

    for part, ref in enumerate(part_refs):
        start = 0
        for cell, white_ref in zip(cells, white_refs):
            rows = part_blocks * cell
            copies = SUB_ROWS // cell
            white = ref[start : start + rows, :].astype(jnp.float32).reshape(rows // SUB_ROWS, SUB_ROWS, width)
            start += rows
            if copies == 1:
                white_ref[part * part_blocks : (part + 1) * part_blocks] = white
            else:
                for sub in range(rows // SUB_ROWS):
                    for copy in range(copies):
                        block = white[sub, copy * cell : (copy + 1) * cell]
                        white_ref[part * part_blocks + sub * copies + copy] = jnp.concatenate([block] * copies, axis=0)
    for white_ref in white_refs:
        white_ref[white_ref.shape[0] - 1] = jnp.zeros((SUB_ROWS, width), jnp.float32)
    sums_ref[...] = jnp.zeros_like(sums_ref)
    sub_row = lax.broadcasted_iota(jnp.int32, (SUB_ROWS, width), 0)

    def pick(white_ref, cell, side, place):
        rows = white_ref[place_ref[side, place]]
        for copy in range(1, SUB_ROWS // cell):
            other = white_ref[place_ref[side, place + copy]]
            rows = jnp.where(sub_row < copy * cell, rows, other)
        return rows

    subs = []
    for index, cell in enumerate(cells):
        subs += [(index, cell, pair) for pair in range(0, unit_pairs, SUB_ROWS // cell)]

    def tile_step(tile, carry):
        for unit in range(tile_units):
            for pack in range(0, len(subs), PACK_ROWS // SUB_ROWS):
                real_parts, imag_parts = [], []
                for index, cell, pair in subs[pack : pack + PACK_ROWS // SUB_ROWS]:
                    place = (tile * tile_units + unit) * unit_pairs + pair
                    first = pick(white_refs[index], cell, 0, place)
                    second = pick(white_refs[index], cell, 1, place)
                    real_a, imag_a = first[:, :num_bins], first[:, num_bins:]
                    real_b, imag_b = second[:, :num_bins], second[:, num_bins:]
                    real_parts.append(real_a * real_b + imag_a * imag_b)
                    imag_parts.append(imag_a * real_b - real_a * imag_b)
                start = unit * unit_rows + pack * SUB_ROWS
                own = slice(start, start + PACK_ROWS)
                real_part = jnp.concatenate(real_parts, axis=0).astype(jnp.bfloat16)
                imag_part = jnp.concatenate(imag_parts, axis=0).astype(jnp.bfloat16)
                for index in range(CLASSES):
                    bins = slice(index * class_bins, (index + 1) * class_bins)
                    middle = (2 * index + 1) * class_bins
                    cross_ref[own, middle - class_bins : middle] = real_part[:, bins]
                    cross_ref[own, middle : middle + class_bins] = imag_part[:, bins]
        for lag in range(quarter // LANES):
            for index in range(CLASSES):
                rows = slice(2 * index * class_bins, 2 * (index + 1) * class_bins)
                lag_ref[lag, index] = jnp.dot(
                    cross_ref[:, rows],
                    table_ref[rows, 2 * lag * LANES : 2 * (lag + 1) * LANES],
                    preferred_element_type=jnp.float32,
                )
        for lag in range(quarter // LANES):
            for unit in range(tile_units):
                group = groups_ref[tile * tile_units + unit]
                totals = [None] * len(cells)
                for sub, (index, _, _) in enumerate(subs):
                    start = unit * unit_rows + sub * SUB_ROWS
                    own = slice(start, start + SUB_ROWS)
                    direct = [lag_ref[lag, k, own, :LANES] for k in range(CLASSES)]
                    quad = [lag_ref[lag, k, own, LANES:] for k in range(CLASSES)]
                    terms = [phase_terms(d, q) for d, q in zip(*quarter_turns(direct, quad))]
                    if totals[index] is None:
                        totals[index] = terms
                    else:
                        totals[index] = [
                            [one + two for one, two in zip(old, new)] for old, new in zip(totals[index], terms)
                        ]
                for index, total in enumerate(totals):
                    for turn_index, kinds in enumerate(total):
                        lags = slice(turn_index * quarter + lag * LANES, turn_index * quarter + (lag + 1) * LANES)
                        for kind, value in enumerate(kinds):
                            sums_ref[kind, group, index, :, lags] += value
        return carry

    lax.fori_loop(0, tiles_ref[0], tile_step, 0)

    linear, coherence = [], []
    for group in range(NGRP):
        scale = norm_ref[group]
        for index, cell in enumerate(cells):
            folded = []
            for kind in range(3):
                whole = sums_ref[kind, group, index]
                total = whole[:cell]
                for start in range(cell, SUB_ROWS, cell):
                    total = total + whole[start : start + cell]
                folded.append(total)
            linear.append(folded[0] * scale)
            coherence.append(jnp.sqrt(folded[1] * folded[1] + folded[2] * folded[2]) * scale)
    smoothed = window_sum(jnp.concatenate(coherence, axis=0)) * (1.0 / (2 * HW + 1))
    stacks = jnp.concatenate(linear, axis=0) * smoothed * smoothed
    pieces, _, piece_lags = out_ref.shape
    for piece in range(pieces):
        out_ref[piece] = stacks[:, piece * piece_lags : (piece + 1) * piece_lags].astype(out_ref.dtype)


def pair_order(pair_blocks, live_pairs, stack_group, parts, part_blocks, unit_pairs, spare_units):
    owners, slots, _ = pair_blocks.shape
    total = owners * slots
    places = (-(-total // unit_pairs) + NGRP + spare_units) * unit_pairs
    group_index = jnp.arange(NGRP, dtype=jnp.int32)
    live = jnp.arange(slots, dtype=jnp.int32)[None, :] < live_pairs[:, None]
    member = (stack_group[:, :, None] == group_index) & live[:, :, None]
    member = member.reshape(total, NGRP).astype(jnp.int32)
    members = jnp.sum(member, axis=0)
    filled = (members + unit_pairs - 1) // unit_pairs * unit_pairs
    ends = jnp.cumsum(filled)
    rank = jnp.cumsum(member, axis=0) - 1
    place = jnp.sum(member * (rank + (ends - filled)[None, :] + 1), axis=1) - 1
    here = jnp.arange(places, dtype=jnp.int32)
    match = here[:, None] == place[None, :]
    me = lax.axis_index("pair")
    blocks = pair_blocks.reshape(total, 2).T
    held = (lax.rem(blocks, parts) ^ me) * part_blocks + blocks // parts
    empty = parts * part_blocks
    taken = jnp.sum(jnp.where(match[None], held[:, None, :] - empty, 0), axis=2) + empty
    unit_start = jnp.arange(places // unit_pairs, dtype=jnp.int32) * unit_pairs
    unit_group = jnp.minimum(jnp.sum((unit_start[:, None] >= ends[None, :]).astype(jnp.int32), axis=1), NGRP - 1)
    norm = 1.0 / jnp.sqrt(members.astype(jnp.float32))
    return ends[-1:] // unit_pairs, taken, unit_group, norm


def chunk_cells(own_channels):
    if own_channels != 2 * SUB_ROWS:
        return [[1] * own_channels]
    return [[8, 4], [4]]


def shards(spectra, pair_blocks, live_pairs, stack_group):
    parts = lax.axis_size("pair")
    me = lax.axis_index("pair")
    cores = lax.axis_size("lag")
    core = lax.axis_index("lag")
    part_blocks, _, channels, width = spectra.shape
    num_bins = width // 2
    lag_count = 2 * num_bins
    own_channels = channels // (parts * cores)
    chunks = chunk_cells(own_channels)
    unit_pairs = PACK_ROWS // min(chunks[-1])
    pieces = parts * cores
    tile_units = [max(1, rows // chunk_rows(cells, unit_pairs)) for cells, rows in zip(chunks, (288, 128))]

    used, taken, unit_group, norm = pair_order(
        pair_blocks, live_pairs, stack_group, parts, part_blocks, unit_pairs, max(tile_units)
    )

    def stack_call(cells, units, received):
        rows = part_blocks * sum(cells)
        if rows % PACK_ROWS:
            received = [jnp.concatenate(received, axis=0)]
        tiles = (used + units - 1) // units
        return pl.pallas_call(
            functools.partial(stack_kernel, len(received), cells, unit_pairs, units),
            out_shape=jax.ShapeDtypeStruct((pieces, NGRP * sum(cells), lag_count // pieces), jnp.float32),
            in_specs=[pl.BlockSpec(memory_space=pltpu.SMEM)] * 4
            + [pl.BlockSpec(memory_space=pltpu.VMEM)] * (len(received) + 1),
            out_specs=pl.BlockSpec(memory_space=pltpu.VMEM),
            scratch_shapes=[
                pltpu.VMEM((parts * part_blocks + 1, SUB_ROWS, width), jnp.float32) for _ in cells
            ]
            + [
                pltpu.VMEM((units * chunk_rows(cells, unit_pairs), width), jnp.bfloat16),
                pltpu.VMEM(
                    (lag_count // CLASSES // LANES, CLASSES, units * chunk_rows(cells, unit_pairs), 2 * LANES),
                    jnp.float32,
                ),
                pltpu.VMEM((3, NGRP, len(cells), SUB_ROWS, lag_count), jnp.float32),
            ],
            compiler_params=pltpu.CompilerParams(vmem_limit_bytes=20 * 1024 * 1024),
            name="stack",
        )(tiles, taken, unit_group, norm, *received, table)

    def move(value, shift):
        return lax.ppermute(value, "pair", [(i, i ^ shift) for i in range(parts)])

    starts = jnp.stack([((me ^ step) * cores + core) * own_channels for step in range(parts)])
    if own_channels % PACK_ROWS == 0:
        shapes = [jax.ShapeDtypeStruct((part_blocks * sum(cells), width), jnp.bfloat16) for cells in chunks]
        flat = pl.pallas_call(
            functools.partial(prepare_kernel, chunks),
            out_shape=shapes * parts,
            in_specs=[pl.BlockSpec(memory_space=pltpu.SMEM), pl.BlockSpec(memory_space=pltpu.HBM)],
            out_specs=[pl.BlockSpec(memory_space=pltpu.VMEM)] * (parts * len(chunks)),
            scratch_shapes=[
                pltpu.VMEM((parts, part_blocks, own_channels, width), jnp.bfloat16),
                pltpu.SemaphoreType.DMA((parts,)),
            ],
            compiler_params=pltpu.CompilerParams(vmem_limit_bytes=16 * 1024 * 1024),
            name="prepare",
        )(starts, spectra)
        pieces_of = [list(flat[index :: len(chunks)]) for index in range(len(chunks))]
    else:
        ordered = whiten(spectra).reshape(part_blocks, channels, 2, num_bins // CLASSES, CLASSES)
        ordered = ordered.swapaxes(3, 4).reshape(part_blocks, channels, width)
        pieces_of = [[]]
        for step in range(parts):
            piece = lax.dynamic_slice_in_dim(ordered, starts[step], own_channels, 1)
            pieces_of[0].append(piece.reshape(part_blocks * own_channels, width))

    received = []
    for index, chunk in enumerate(pieces_of):
        if index == 1:
            chunk[1:], received[0][2] = lax.optimization_barrier((chunk[1:], received[0][2]))
        received.append([chunk[0]] + [move(chunk[step], step) for step in range(1, parts)])
        if index == 0:
            used, received[0][2] = lax.optimization_barrier((used, received[0][2]))
            table = lag_table(used, lag_count, num_bins)
    stacks = [stack_call(cells, units, got) for cells, units, got in zip(chunks, tile_units, received)]

    stacks = jnp.concatenate(stacks, axis=1).astype(jnp.bfloat16)
    rows = stacks.shape[1]
    if cores == 2:
        stacks = stacks.reshape(parts, cores, rows, -1)
        mine = lax.dynamic_index_in_dim(stacks, core, 1, keepdims=False)
        other = lax.dynamic_index_in_dim(stacks, 1 - core, 1, keepdims=False)
        other = lax.ppermute(other, "lag", [(0, 1), (1, 0)])
        both = jnp.where(core == 0, jnp.stack([mine, other], 1), jnp.stack([other, mine], 1))
        got = []
        for step in range(parts):
            part = lax.dynamic_index_in_dim(both, me ^ step, 0, keepdims=False)
            got.append(move(part, step) if step else part)
        got = jnp.stack(got)[me ^ jnp.arange(parts, dtype=jnp.int32)]
    else:
        got = lax.all_to_all(stacks, ("pair", "lag"), 0, 0, tiled=True)
    got = got.reshape(pieces, rows, -1)
    blocks = []
    offset = 0
    for cell in map(sum, chunks):
        block = got[:, offset : offset + NGRP * cell].reshape(pieces, NGRP, cell, -1)
        blocks.append(block)
        offset += NGRP * cell
    whole = jnp.concatenate(blocks, axis=2)
    return whole.transpose(1, 0, 2, 3).reshape(NGRP, channels, -1).astype(jnp.float32)


def solution(mesh):
    return jax.shard_map(
        shards,
        mesh=mesh,
        in_specs=(P("win", "pair", "stk", None), P("win", None, None), P("win"), P("win", None)),
        out_specs=P("win", "stk", ("pair", "lag")),
        check_vma=False,
    )
```

```python
import functools
import math

import jax
import jax.numpy as jnp
from jax import lax
from jax.experimental import pallas as pl
from jax.experimental.pallas import tpu as pltpu
from jax.sharding import PartitionSpec as P

NGRP = 4
HW = 15

AMP_FLOOR = 0.5
EPSILON = 1e-06
TILE_ROWS = 256
PACK_ROWS = 16
SUB_ROWS = 8
LANES = 128
CLASSES = 4


def turn(steps, period):
    quarter = period // 4
    quadrant = (steps + quarter // 2) // quarter
    angle = (steps - quadrant * quarter).astype(jnp.float32) * (2.0 * math.pi / period)
    square = angle * angle
    cosine = 1.0 + square * (-1 / 2 + square * (1 / 24 + square * (-1 / 720 + square * (1 / 40320))))
    sine = angle * (1.0 + square * (-1 / 6 + square * (1 / 120 + square * (-1 / 5040 + square * (1 / 362880)))))
    odd = (quadrant & 1) == 1
    cosine, sine = jnp.where(odd, sine, cosine), jnp.where(odd, cosine, sine)
    cosine = jnp.where(((quadrant + 1) & 2) == 2, -cosine, cosine)
    sine = jnp.where((quadrant & 2) == 2, -sine, sine)
    return cosine, sine


def table_kernel(used_ref, out_ref):
    width, columns = out_ref.shape
    num_bins = width // 2
    period = 2 * num_bins
    scale = math.sqrt(2.0 / num_bins)
    class_bins = num_bins // CLASSES
    rows = lax.broadcasted_iota(jnp.int32, (class_bins, LANES), 0)
    lanes = lax.broadcasted_iota(jnp.int32, (class_bins, LANES), 1)
    for index in range(CLASSES):
        real_rows = slice(2 * index * class_bins, (2 * index + 1) * class_bins)
        imag_rows = slice((2 * index + 1) * class_bins, (2 * index + 2) * class_bins)
        for tile in range(columns // (2 * LANES)):
            lags = lanes + (tile * LANES + num_bins)
            cosine, sine = turn((rows * CLASSES + index) * lags & (period - 1), period)
            cosine, sine = cosine * scale, sine * scale
            direct = slice(2 * tile * LANES, (2 * tile + 1) * LANES)
            quad = slice((2 * tile + 1) * LANES, (2 * tile + 2) * LANES)
            out_ref[real_rows, direct] = cosine.astype(jnp.bfloat16)
            out_ref[imag_rows, direct] = (-sine).astype(jnp.bfloat16)
            out_ref[real_rows, quad] = sine.astype(jnp.bfloat16)
            out_ref[imag_rows, quad] = cosine.astype(jnp.bfloat16)


def lag_table(used, lag_count, num_bins):
    return pl.pallas_call(
        table_kernel,
        out_shape=jax.ShapeDtypeStruct((2 * num_bins, 2 * lag_count // CLASSES), jnp.bfloat16),
        in_specs=[pl.BlockSpec(memory_space=pltpu.SMEM)],
        out_specs=pl.BlockSpec(memory_space=pltpu.VMEM),
        compiler_params=pltpu.CompilerParams(vmem_limit_bytes=6 * 1024 * 1024),
        name="table",
    )(used)


def whiten(values):
    values = values.astype(jnp.float32)
    power = jnp.sum(values * values, axis=-1, keepdims=True) * (2.0 / values.shape[-1])
    return (values * lax.rsqrt(power + EPSILON)).astype(jnp.bfloat16)


def prepare_kernel(chunks, wanted, *refs):
    order = list(dict.fromkeys(step for step, _ in wanted))
    raw_refs = dict(zip(order, refs))
    out_refs = dict(zip(wanted, refs[len(order) :]))
    blocks, _, own_channels, width = refs[0].shape
    num_bins = width // 2
    class_bins = num_bins // CLASSES
    source = lax.broadcasted_iota(jnp.int32, (num_bins, num_bins), 0)
    target = lax.broadcasted_iota(jnp.int32, (num_bins, num_bins), 1)
    moved = (target & (class_bins - 1)) * CLASSES + target // class_bins
    shuffle = jnp.where(source == moved, 1.0, 0.0).astype(jnp.bfloat16)
    for step in order:
        white = whiten(raw_refs[step][...].reshape(blocks * own_channels, width))
        halves = [
            jnp.dot(white[:, start : start + num_bins], shuffle, preferred_element_type=jnp.float32)
            for start in (0, num_bins)
        ]
        halves = [half.reshape(blocks, own_channels, num_bins) for half in halves]
        offset = 0
        for index, cells in enumerate(chunks):
            if (step, index) not in out_refs:
                offset += sum(cells)
                continue
            out_ref = out_refs[step, index]
            row = 0
            for cell in cells:
                group = SUB_ROWS // cell
                for block in range(0, blocks, 2 * group):
                    for side, half in enumerate(halves):
                        rows = [half[block + k, offset : offset + cell] for k in range(2 * group)]
                        rows = jnp.concatenate(rows, axis=0).astype(jnp.bfloat16)
                        out_ref[row : row + PACK_ROWS, side * num_bins : (side + 1) * num_bins] = rows
                    row += PACK_ROWS
                offset += cell


def window_sum(values):
    rows, lags = values.shape
    edge = jnp.zeros((rows, 128), jnp.float32)
    one = jnp.concatenate([edge, values, edge], axis=1)
    width = one.shape[1]
    two = one + pltpu.roll(one, 1, 1)
    four = two + pltpu.roll(two, 2, 1)
    eight = four + pltpu.roll(four, 4, 1)
    back = eight + pltpu.roll(eight, 8, 1)
    ahead = eight + pltpu.roll(four, 8, 1) + pltpu.roll(two, 12, 1) + pltpu.roll(one, 14, 1)
    return (back + pltpu.roll(ahead, width - HW, 1))[:, 128 : 128 + lags]


def chunk_rows(cells, unit_pairs):
    return unit_pairs * sum(cells)


def quarter_turns(direct, quad):
    even_d, even_q = direct[0] + direct[2], quad[0] + quad[2]
    odd_d, odd_q = direct[1] + direct[3], quad[1] + quad[3]
    even_e, even_r = direct[0] - direct[2], quad[0] - quad[2]
    odd_e, odd_r = direct[1] - direct[3], quad[1] - quad[3]
    return (
        [even_d + odd_d, even_e - odd_r, even_d - odd_d, even_e + odd_r],
        [even_q + odd_q, even_r + odd_e, even_q - odd_q, even_r - odd_e],
    )


def phase_terms(direct, quad):
    inverse = jnp.minimum(lax.rsqrt(direct * direct + quad * quad), 1.0 / AMP_FLOOR)
    return [direct, direct * inverse, quad * inverse]


def stack_kernel(num_parts, cells, unit_pairs, tile_units, num_done, tiles_ref, place_ref, groups_ref, norm_ref, *refs):
    refs = list(refs)
    part_refs = [refs.pop(0) for _ in range(num_parts)]
    table_ref = refs.pop(0)
    if num_done:
        piece_ref = refs.pop(0)
        done_refs = [refs.pop(0) for _ in range(num_done)]
        near_ref, far_ref = refs.pop(0), refs.pop(0)
    else:
        out_ref = refs.pop(0)
    white_refs = [refs.pop(0) for _ in cells]
    cross_ref, lag_ref, sums_ref = refs[:3]
    part_rows, width = part_refs[0].shape
    num_bins = width // 2
    class_bins = num_bins // CLASSES
    quarter = width // CLASSES
    unit_rows = chunk_rows(cells, unit_pairs)
    part_blocks = part_rows // sum(cells)

    for part, ref in enumerate(part_refs):
        start = 0
        for cell, white_ref in zip(cells, white_refs):
            rows = part_blocks * cell
            copies = SUB_ROWS // cell
            white = ref[start : start + rows, :].astype(jnp.float32).reshape(rows // SUB_ROWS, SUB_ROWS, width)
            start += rows
            if copies == 1:
                white_ref[part * part_blocks : (part + 1) * part_blocks] = white
            else:
                for sub in range(rows // SUB_ROWS):
                    for copy in range(copies):
                        block = white[sub, copy * cell : (copy + 1) * cell]
                        white_ref[part * part_blocks + sub * copies + copy] = jnp.concatenate([block] * copies, axis=0)
    for white_ref in white_refs:
        white_ref[white_ref.shape[0] - 1] = jnp.zeros((SUB_ROWS, width), jnp.float32)
    sums_ref[...] = jnp.zeros_like(sums_ref)
    sub_row = lax.broadcasted_iota(jnp.int32, (SUB_ROWS, width), 0)

    def pick(white_ref, cell, side, place):
        rows = white_ref[place_ref[side, place]]
        for copy in range(1, SUB_ROWS // cell):
            other = white_ref[place_ref[side, place + copy]]
            rows = jnp.where(sub_row < copy * cell, rows, other)
        return rows

    subs = []
    for index, cell in enumerate(cells):
        subs += [(index, cell, pair) for pair in range(0, unit_pairs, SUB_ROWS // cell)]

    def tile_step(tile, carry):
        for unit in range(tile_units):
            for pack in range(0, len(subs), PACK_ROWS // SUB_ROWS):
                real_parts, imag_parts = [], []
                for index, cell, pair in subs[pack : pack + PACK_ROWS // SUB_ROWS]:
                    place = (tile * tile_units + unit) * unit_pairs + pair
                    first = pick(white_refs[index], cell, 0, place)
                    second = pick(white_refs[index], cell, 1, place)
                    real_a, imag_a = first[:, :num_bins], first[:, num_bins:]
                    real_b, imag_b = second[:, :num_bins], second[:, num_bins:]
                    real_parts.append(real_a * real_b + imag_a * imag_b)
                    imag_parts.append(imag_a * real_b - real_a * imag_b)
                start = unit * unit_rows + pack * SUB_ROWS
                own = slice(start, start + PACK_ROWS)
                real_part = jnp.concatenate(real_parts, axis=0).astype(jnp.bfloat16)
                imag_part = jnp.concatenate(imag_parts, axis=0).astype(jnp.bfloat16)
                for index in range(CLASSES):
                    bins = slice(index * class_bins, (index + 1) * class_bins)
                    middle = (2 * index + 1) * class_bins
                    cross_ref[own, middle - class_bins : middle] = real_part[:, bins]
                    cross_ref[own, middle : middle + class_bins] = imag_part[:, bins]
        for lag in range(quarter // LANES):
            for index in range(CLASSES):
                rows = slice(2 * index * class_bins, 2 * (index + 1) * class_bins)
                lag_ref[lag, index] = jnp.dot(
                    cross_ref[:, rows],
                    table_ref[rows, 2 * lag * LANES : 2 * (lag + 1) * LANES],
                    preferred_element_type=jnp.float32,
                )
        for lag in range(quarter // LANES):
            for unit in range(tile_units):
                group = groups_ref[tile * tile_units + unit]
                totals = [None] * len(cells)
                for sub, (index, _, _) in enumerate(subs):
                    start = unit * unit_rows + sub * SUB_ROWS
                    own = slice(start, start + SUB_ROWS)
                    direct = [lag_ref[lag, k, own, :LANES] for k in range(CLASSES)]
                    quad = [lag_ref[lag, k, own, LANES:] for k in range(CLASSES)]
                    terms = [phase_terms(d, q) for d, q in zip(*quarter_turns(direct, quad))]
                    if totals[index] is None:
                        totals[index] = terms
                    else:
                        totals[index] = [
                            [one + two for one, two in zip(old, new)] for old, new in zip(totals[index], terms)
                        ]
                for index, total in enumerate(totals):
                    for turn_index, kinds in enumerate(total):
                        lags = slice(turn_index * quarter + lag * LANES, turn_index * quarter + (lag + 1) * LANES)
                        for kind, value in enumerate(kinds):
                            sums_ref[kind, group, index, :, lags] += value
        return carry

    lax.fori_loop(0, tiles_ref[0], tile_step, 0)

    linear, coherence = [], []
    for group in range(NGRP):
        scale = norm_ref[group]
        for index, cell in enumerate(cells):
            folded = []
            for kind in range(3):
                whole = sums_ref[kind, group, index]
                total = whole[:cell]
                for start in range(cell, SUB_ROWS, cell):
                    total = total + whole[start : start + cell]
                folded.append(total)
            linear.append(folded[0] * scale)
            coherence.append(jnp.sqrt(folded[1] * folded[1] + folded[2] * folded[2]) * scale)
    smoothed = window_sum(jnp.concatenate(coherence, axis=0)) * (1.0 / (2 * HW + 1))
    stacks = jnp.concatenate(linear, axis=0) * smoothed * smoothed
    channels = sum(cells)
    if not num_done:
        for group in range(NGRP):
            out_ref[group] = stacks[group * channels : (group + 1) * channels]
        return
    whole_ref = refs[3]
    for group in range(NGRP):
        rows = [ref[group] for ref in done_refs] + [stacks[group * channels : (group + 1) * channels]]
        rows = jnp.concatenate(rows, axis=0)
        whole_ref[group * rows.shape[0] : (group + 1) * rows.shape[0], :] = rows
    parts, _, piece_lags = near_ref.shape
    for step in range(parts):
        for flip, out_ref in enumerate((near_ref, far_ref)):
            piece = piece_ref[0] ^ (2 * step + flip)
            lags = pl.ds(pl.multiple_of(piece * piece_lags, LANES), piece_lags)
            out_ref[step] = whole_ref[:, lags].astype(out_ref.dtype)


def place_kernel(piece_ref, *refs):
    *step_refs, out_ref, held_ref = refs
    for step, ref in enumerate(step_refs):
        held_ref[2 * step : 2 * step + 2] = ref[...]
    pieces = held_ref.shape[0]
    cell = held_ref.shape[1] // NGRP
    for source in range(pieces):
        block = held_ref[piece_ref[0] ^ source].astype(jnp.float32)
        for group in range(NGRP):
            out_ref[group, source * cell : (source + 1) * cell, :] = block[group * cell : (group + 1) * cell]


def pair_order(pair_blocks, live_pairs, stack_group, parts, part_blocks, unit_pairs, spare_units):
    owners, slots, _ = pair_blocks.shape
    total = owners * slots
    places = (-(-total // unit_pairs) + NGRP + spare_units) * unit_pairs
    group_index = jnp.arange(NGRP, dtype=jnp.int32)
    live = jnp.arange(slots, dtype=jnp.int32)[None, :] < live_pairs[:, None]
    member = (stack_group[:, :, None] == group_index) & live[:, :, None]
    member = member.reshape(total, NGRP).astype(jnp.int32)
    members = jnp.sum(member, axis=0)
    filled = (members + unit_pairs - 1) // unit_pairs * unit_pairs
    ends = jnp.cumsum(filled)
    rank = jnp.cumsum(member, axis=0) - 1
    place = jnp.sum(member * (rank + (ends - filled)[None, :] + 1), axis=1) - 1
    here = jnp.arange(places, dtype=jnp.int32)
    match = here[:, None] == place[None, :]
    me = lax.axis_index("pair")
    blocks = pair_blocks.reshape(total, 2).T
    held = (lax.rem(blocks, parts) ^ me) * part_blocks + blocks // parts
    empty = parts * part_blocks
    taken = jnp.sum(jnp.where(match[None], held[:, None, :] - empty, 0), axis=2) + empty
    unit_start = jnp.arange(places // unit_pairs, dtype=jnp.int32) * unit_pairs
    unit_group = jnp.minimum(jnp.sum((unit_start[:, None] >= ends[None, :]).astype(jnp.int32), axis=1), NGRP - 1)
    norm = 1.0 / jnp.sqrt(members.astype(jnp.float32))
    return ends[-1:] // unit_pairs, taken, unit_group, norm


def chunk_cells(own_channels, parts, cores):
    if (own_channels, parts, cores) != (2 * SUB_ROWS, 4, 2):
        return [[1] * own_channels]
    return [[8], [4], [4]]


def shards(spectra, pair_blocks, live_pairs, stack_group):
    parts = lax.axis_size("pair")
    me = lax.axis_index("pair")
    cores = lax.axis_size("lag")
    core = lax.axis_index("lag")
    part_blocks, _, channels, width = spectra.shape
    num_bins = width // 2
    lag_count = 2 * num_bins
    own_channels = channels // (parts * cores)
    chunks = chunk_cells(own_channels, parts, cores)
    unit_pairs = PACK_ROWS // min(chunks[-1])
    pieces = parts * cores
    here = (me * cores + core).reshape(1)
    tile_units = [max(1, rows // chunk_rows(cells, unit_pairs)) for cells, rows in zip(chunks, (256, 128, 128))]

    used, taken, unit_group, norm = pair_order(
        pair_blocks, live_pairs, stack_group, parts, part_blocks, unit_pairs, max(tile_units)
    )

    def stack_call(cells, units, received, done):
        rows = part_blocks * sum(cells)
        if rows % PACK_ROWS:
            received = [jnp.concatenate(received, axis=0)]
        tiles = (used + units - 1) // units
        smem, vmem = pl.BlockSpec(memory_space=pltpu.SMEM), pl.BlockSpec(memory_space=pltpu.VMEM)
        tile_rows = units * chunk_rows(cells, unit_pairs)
        in_specs = [smem] * 4 + [vmem] * (len(received) + 1)
        args = [tiles, taken, unit_group, norm, *received, table]
        out_shape = jax.ShapeDtypeStruct((NGRP, sum(cells), lag_count), jnp.float32)
        scratch = [pltpu.VMEM((parts * part_blocks + 1, SUB_ROWS, width), jnp.float32) for _ in cells]
        scratch += [
            pltpu.VMEM((tile_rows, width), jnp.bfloat16),
            pltpu.VMEM((lag_count // CLASSES // LANES, CLASSES, tile_rows, 2 * LANES), jnp.float32),
            pltpu.VMEM((3, NGRP, len(cells), SUB_ROWS, lag_count), jnp.float32),
        ]
        out_specs = vmem
        if done:
            in_specs += [smem] + [vmem] * len(done)
            args += [here, *done]
            piece = jax.ShapeDtypeStruct((parts, NGRP * own_channels, lag_count // pieces), jnp.bfloat16)
            out_shape, out_specs = [piece, piece], [vmem, vmem]
            scratch.append(pltpu.VMEM((NGRP * own_channels, lag_count), jnp.float32))
        return pl.pallas_call(
            functools.partial(stack_kernel, len(received), cells, unit_pairs, units, len(done)),
            out_shape=out_shape,
            in_specs=in_specs,
            out_specs=out_specs,
            scratch_shapes=scratch,
            compiler_params=pltpu.CompilerParams(vmem_limit_bytes=20 * 1024 * 1024),
            name="stack",
        )(*args)

    def move(value, shift):
        return lax.ppermute(value, "pair", [(i, i ^ shift) for i in range(parts)])

    starts = [((me ^ step) * cores + core) * own_channels for step in range(parts)]
    if len(chunks) > 1:
        pieces_of = [[None] * parts for _ in chunks]
        raw = {}
        calls = [[(2, 0)], [(3, 0), (1, 0)], [(0, 0)] + [(step, index) for index in range(1, len(chunks)) for step in range(parts)]]
        for wanted in calls:
            steps = list(dict.fromkeys(step for step, _ in wanted))
            for step in steps:
                if step not in raw:
                    raw[step] = lax.dynamic_slice_in_dim(spectra, starts[step], own_channels, 2)
            flat = pl.pallas_call(
                functools.partial(prepare_kernel, chunks, wanted),
                out_shape=[
                    jax.ShapeDtypeStruct((part_blocks * sum(chunks[index]), width), jnp.bfloat16)
                    for _, index in wanted
                ],
                in_specs=[pl.BlockSpec(memory_space=pltpu.VMEM)] * len(steps),
                out_specs=[pl.BlockSpec(memory_space=pltpu.VMEM)] * len(wanted),
                compiler_params=pltpu.CompilerParams(vmem_limit_bytes=16 * 1024 * 1024),
                name="prepare",
            )(*[raw[step] for step in steps])
            flat = list(flat)
            flat[0], starts = lax.optimization_barrier((flat[0], starts))
            for (step, index), piece in zip(wanted, flat):
                pieces_of[index][step] = piece
    else:
        ordered = whiten(spectra).reshape(part_blocks, channels, 2, num_bins // CLASSES, CLASSES)
        ordered = ordered.swapaxes(3, 4).reshape(part_blocks, channels, width)
        pieces_of = [[]]
        for step in range(parts):
            piece = lax.dynamic_slice_in_dim(ordered, starts[step], own_channels, 1)
            pieces_of[0].append(piece.reshape(part_blocks * own_channels, width))

    received, done = [], []
    for index, (cells, units, chunk) in enumerate(zip(chunks, tile_units, pieces_of)):
        if index == 1:
            chunk[1:], received[0][2] = lax.optimization_barrier((chunk[1:], received[0][2]))
        if index > 1:
            chunk[1:], done[index - 2] = lax.optimization_barrier((chunk[1:], done[index - 2]))
        received.append([chunk[0]] + [move(chunk[step], step) for step in range(1, parts)])
        if index == 0:
            if parts > 2:
                used, received[0][2] = lax.optimization_barrier((used, received[0][2]))
            table = lag_table(used, lag_count, num_bins)
        if len(chunks) == 1:
            return lax.all_to_all(stack_call(cells, units, received[0], []), ("pair", "lag"), 2, 1, tiled=True)
        if index < len(chunks) - 1:
            done.append(stack_call(cells, units, received[index], []))

    near, far = stack_call(chunks[-1], tile_units[-1], received[-1], done)
    other = lax.ppermute(far, "lag", [(i, i ^ 1) for i in range(cores)])
    both = jnp.stack([near, other], 1)
    arrived = [both[0]] + [move(both[step], step) for step in range(1, parts)]
    return pl.pallas_call(
        place_kernel,
        out_shape=jax.ShapeDtypeStruct((NGRP, channels, lag_count // pieces), jnp.float32),
        in_specs=[pl.BlockSpec(memory_space=pltpu.SMEM)] + [pl.BlockSpec(memory_space=pltpu.VMEM)] * parts,
        out_specs=pl.BlockSpec(memory_space=pltpu.VMEM),
        scratch_shapes=[pltpu.VMEM((pieces, NGRP * own_channels, lag_count // pieces), jnp.bfloat16)],
        compiler_params=pltpu.CompilerParams(vmem_limit_bytes=8 * 1024 * 1024),
        name="place",
    )(here, *arrived)


def solution(mesh):
    return jax.shard_map(
        shards,
        mesh=mesh,
        in_specs=(P("win", "pair", "stk", None), P("win", None, None), P("win"), P("win", None)),
        out_specs=P("win", "stk", ("pair", "lag")),
        check_vma=False,
    )
```

```python
import functools
import math

import jax
import jax.numpy as jnp
from jax import lax
from jax.experimental import pallas as pl
from jax.experimental.pallas import tpu as pltpu
from jax.sharding import PartitionSpec as P

NGRP = 4
HW = 15

AMP_FLOOR = 0.5
EPSILON = 1e-06
TILE_ROWS = 256
PACK_ROWS = 16
SUB_ROWS = 8
LANES = 128
CLASSES = 4


def turn(steps, period):
    quarter = period // 4
    quadrant = (steps + quarter // 2) // quarter
    angle = (steps - quadrant * quarter).astype(jnp.float32) * (2.0 * math.pi / period)
    square = angle * angle
    cosine = 1.0 + square * (-1 / 2 + square * (1 / 24 + square * (-1 / 720 + square * (1 / 40320))))
    sine = angle * (1.0 + square * (-1 / 6 + square * (1 / 120 + square * (-1 / 5040 + square * (1 / 362880)))))
    odd = (quadrant & 1) == 1
    cosine, sine = jnp.where(odd, sine, cosine), jnp.where(odd, cosine, sine)
    cosine = jnp.where(((quadrant + 1) & 2) == 2, -cosine, cosine)
    sine = jnp.where((quadrant & 2) == 2, -sine, sine)
    return cosine, sine


def table_kernel(used_ref, out_ref):
    width, columns = out_ref.shape
    num_bins = width // 2
    period = 2 * num_bins
    scale = math.sqrt(2.0 / num_bins)
    class_bins = num_bins // CLASSES
    rows = lax.broadcasted_iota(jnp.int32, (class_bins, LANES), 0)
    lanes = lax.broadcasted_iota(jnp.int32, (class_bins, LANES), 1)
    for index in range(CLASSES):
        real_rows = slice(2 * index * class_bins, (2 * index + 1) * class_bins)
        imag_rows = slice((2 * index + 1) * class_bins, (2 * index + 2) * class_bins)
        for tile in range(columns // (2 * LANES)):
            lags = lanes + (tile * LANES + num_bins)
            cosine, sine = turn((rows * CLASSES + index) * lags & (period - 1), period)
            cosine, sine = cosine * scale, sine * scale
            direct = slice(2 * tile * LANES, (2 * tile + 1) * LANES)
            quad = slice((2 * tile + 1) * LANES, (2 * tile + 2) * LANES)
            out_ref[real_rows, direct] = cosine.astype(jnp.bfloat16)
            out_ref[imag_rows, direct] = (-sine).astype(jnp.bfloat16)
            out_ref[real_rows, quad] = sine.astype(jnp.bfloat16)
            out_ref[imag_rows, quad] = cosine.astype(jnp.bfloat16)


def lag_table(used, lag_count, num_bins):
    return pl.pallas_call(
        table_kernel,
        out_shape=jax.ShapeDtypeStruct((2 * num_bins, 2 * lag_count // CLASSES), jnp.bfloat16),
        in_specs=[pl.BlockSpec(memory_space=pltpu.SMEM)],
        out_specs=pl.BlockSpec(memory_space=pltpu.VMEM),
        compiler_params=pltpu.CompilerParams(vmem_limit_bytes=6 * 1024 * 1024),
        name="table",
    )(used)


def whiten(values):
    values = values.astype(jnp.float32)
    power = jnp.sum(values * values, axis=-1, keepdims=True) * (2.0 / values.shape[-1])
    return (values * lax.rsqrt(power + EPSILON)).astype(jnp.bfloat16)


def prepare_kernel(chunks, wanted, *refs):
    order = list(dict.fromkeys(step for step, _ in wanted))
    raw_refs = dict(zip(order, refs))
    out_refs = dict(zip(wanted, refs[len(order) :]))
    blocks, _, own_channels, width = refs[0].shape
    num_bins = width // 2
    class_bins = num_bins // CLASSES
    source = lax.broadcasted_iota(jnp.int32, (num_bins, num_bins), 0)
    target = lax.broadcasted_iota(jnp.int32, (num_bins, num_bins), 1)
    moved = (target & (class_bins - 1)) * CLASSES + target // class_bins
    shuffle = jnp.where(source == moved, 1.0, 0.0).astype(jnp.bfloat16)
    for step in order:
        white = whiten(raw_refs[step][...].reshape(blocks * own_channels, width))
        halves = [
            jnp.dot(white[:, start : start + num_bins], shuffle, preferred_element_type=jnp.float32)
            for start in (0, num_bins)
        ]
        halves = [half.reshape(blocks, own_channels, num_bins) for half in halves]
        offset = 0
        for index, cells in enumerate(chunks):
            if (step, index) not in out_refs:
                offset += sum(cells)
                continue
            out_ref = out_refs[step, index]
            row = 0
            for cell in cells:
                group = SUB_ROWS // cell
                for block in range(0, blocks, 2 * group):
                    for side, half in enumerate(halves):
                        rows = [half[block + k, offset : offset + cell] for k in range(2 * group)]
                        rows = jnp.concatenate(rows, axis=0).astype(jnp.bfloat16)
                        out_ref[row : row + PACK_ROWS, side * num_bins : (side + 1) * num_bins] = rows
                    row += PACK_ROWS
                offset += cell


def window_sum(values):
    rows, lags = values.shape
    edge = jnp.zeros((rows, 128), jnp.float32)
    one = jnp.concatenate([edge, values, edge], axis=1)
    width = one.shape[1]
    two = one + pltpu.roll(one, 1, 1)
    four = two + pltpu.roll(two, 2, 1)
    eight = four + pltpu.roll(four, 4, 1)
    back = eight + pltpu.roll(eight, 8, 1)
    ahead = eight + pltpu.roll(four, 8, 1) + pltpu.roll(two, 12, 1) + pltpu.roll(one, 14, 1)
    return (back + pltpu.roll(ahead, width - HW, 1))[:, 128 : 128 + lags]


def chunk_rows(cells, unit_pairs):
    return unit_pairs * sum(cells)


def quarter_turns(direct, quad):
    even_d, even_q = direct[0] + direct[2], quad[0] + quad[2]
    odd_d, odd_q = direct[1] + direct[3], quad[1] + quad[3]
    even_e, even_r = direct[0] - direct[2], quad[0] - quad[2]
    odd_e, odd_r = direct[1] - direct[3], quad[1] - quad[3]
    return (
        [even_d + odd_d, even_e - odd_r, even_d - odd_d, even_e + odd_r],
        [even_q + odd_q, even_r + odd_e, even_q - odd_q, even_r - odd_e],
    )


def phase_terms(direct, quad):
    inverse = jnp.minimum(lax.rsqrt(direct * direct + quad * quad), 1.0 / AMP_FLOOR)
    return [direct, direct * inverse, quad * inverse]


def stack_kernel(num_parts, cells, unit_pairs, tile_units, num_done, tiles_ref, place_ref, groups_ref, norm_ref, *refs):
    refs = list(refs)
    part_refs = [refs.pop(0) for _ in range(num_parts)]
    table_ref = refs.pop(0)
    if num_done:
        piece_ref = refs.pop(0)
        done_refs = [refs.pop(0) for _ in range(num_done)]
        near_ref, far_ref = refs.pop(0), refs.pop(0)
    else:
        out_ref = refs.pop(0)
    white_refs = [refs.pop(0) for _ in cells]
    cross_ref, lag_ref, sums_ref = refs[:3]
    part_rows, width = part_refs[0].shape
    num_bins = width // 2
    class_bins = num_bins // CLASSES
    quarter = width // CLASSES
    unit_rows = chunk_rows(cells, unit_pairs)
    part_blocks = part_rows // sum(cells)

    for part, ref in enumerate(part_refs):
        start = 0
        for cell, white_ref in zip(cells, white_refs):
            rows = part_blocks * cell
            copies = SUB_ROWS // cell
            white = ref[start : start + rows, :].astype(jnp.float32).reshape(rows // SUB_ROWS, SUB_ROWS, width)
            start += rows
            if copies == 1:
                white_ref[part * part_blocks : (part + 1) * part_blocks] = white
            else:
                for sub in range(rows // SUB_ROWS):
                    for copy in range(copies):
                        block = white[sub, copy * cell : (copy + 1) * cell]
                        white_ref[part * part_blocks + sub * copies + copy] = jnp.concatenate([block] * copies, axis=0)
    for white_ref in white_refs:
        white_ref[white_ref.shape[0] - 1] = jnp.zeros((SUB_ROWS, width), jnp.float32)
    sums_ref[...] = jnp.zeros_like(sums_ref)
    sub_row = lax.broadcasted_iota(jnp.int32, (SUB_ROWS, width), 0)

    def pick(white_ref, cell, side, place):
        rows = white_ref[place_ref[side, place]]
        for copy in range(1, SUB_ROWS // cell):
            other = white_ref[place_ref[side, place + copy]]
            rows = jnp.where(sub_row < copy * cell, rows, other)
        return rows

    subs = []
    for index, cell in enumerate(cells):
        subs += [(index, cell, pair) for pair in range(0, unit_pairs, SUB_ROWS // cell)]

    def tile_step(tile, carry):
        for unit in range(tile_units):
            for pack in range(0, len(subs), PACK_ROWS // SUB_ROWS):
                real_parts, imag_parts = [], []
                for index, cell, pair in subs[pack : pack + PACK_ROWS // SUB_ROWS]:
                    place = (tile * tile_units + unit) * unit_pairs + pair
                    first = pick(white_refs[index], cell, 0, place)
                    second = pick(white_refs[index], cell, 1, place)
                    real_a, imag_a = first[:, :num_bins], first[:, num_bins:]
                    real_b, imag_b = second[:, :num_bins], second[:, num_bins:]
                    real_parts.append(real_a * real_b + imag_a * imag_b)
                    imag_parts.append(imag_a * real_b - real_a * imag_b)
                start = unit * unit_rows + pack * SUB_ROWS
                own = slice(start, start + PACK_ROWS)
                real_part = jnp.concatenate(real_parts, axis=0).astype(jnp.bfloat16)
                imag_part = jnp.concatenate(imag_parts, axis=0).astype(jnp.bfloat16)
                for index in range(CLASSES):
                    bins = slice(index * class_bins, (index + 1) * class_bins)
                    middle = (2 * index + 1) * class_bins
                    cross_ref[own, middle - class_bins : middle] = real_part[:, bins]
                    cross_ref[own, middle : middle + class_bins] = imag_part[:, bins]
        for lag in range(quarter // LANES):
            for index in range(CLASSES):
                rows = slice(2 * index * class_bins, 2 * (index + 1) * class_bins)
                lag_ref[lag, index] = jnp.dot(
                    cross_ref[:, rows],
                    table_ref[rows, 2 * lag * LANES : 2 * (lag + 1) * LANES],
                    preferred_element_type=jnp.float32,
                )
        for lag in range(quarter // LANES):
            for unit in range(tile_units):
                group = groups_ref[tile * tile_units + unit]
                totals = [None] * len(cells)
                for sub, (index, _, _) in enumerate(subs):
                    start = unit * unit_rows + sub * SUB_ROWS
                    own = slice(start, start + SUB_ROWS)
                    direct = [lag_ref[lag, k, own, :LANES] for k in range(CLASSES)]
                    quad = [lag_ref[lag, k, own, LANES:] for k in range(CLASSES)]
                    terms = [phase_terms(d, q) for d, q in zip(*quarter_turns(direct, quad))]
                    if totals[index] is None:
                        totals[index] = terms
                    else:
                        totals[index] = [
                            [one + two for one, two in zip(old, new)] for old, new in zip(totals[index], terms)
                        ]
                for index, total in enumerate(totals):
                    for turn_index, kinds in enumerate(total):
                        lags = slice(turn_index * quarter + lag * LANES, turn_index * quarter + (lag + 1) * LANES)
                        for kind, value in enumerate(kinds):
                            sums_ref[kind, group, index, :, lags] += value
        return carry

    lax.fori_loop(0, tiles_ref[0], tile_step, 0)

    linear, coherence = [], []
    for group in range(NGRP):
        scale = norm_ref[group]
        for index, cell in enumerate(cells):
            folded = []
            for kind in range(3):
                whole = sums_ref[kind, group, index]
                total = whole[:cell]
                for start in range(cell, SUB_ROWS, cell):
                    total = total + whole[start : start + cell]
                folded.append(total)
            linear.append(folded[0] * scale)
            coherence.append(jnp.sqrt(folded[1] * folded[1] + folded[2] * folded[2]) * scale)
    smoothed = window_sum(jnp.concatenate(coherence, axis=0)) * (1.0 / (2 * HW + 1))
    stacks = jnp.concatenate(linear, axis=0) * smoothed * smoothed
    channels = sum(cells)
    if not num_done:
        for group in range(NGRP):
            out_ref[group] = stacks[group * channels : (group + 1) * channels]
        return
    whole_ref = refs[3]
    for group in range(NGRP):
        rows = [ref[group] for ref in done_refs] + [stacks[group * channels : (group + 1) * channels]]
        rows = jnp.concatenate(rows, axis=0)
        whole_ref[group * rows.shape[0] : (group + 1) * rows.shape[0], :] = rows
    parts, _, piece_lags = near_ref.shape
    for step in range(parts):
        for flip, out_ref in enumerate((near_ref, far_ref)):
            piece = piece_ref[0] ^ (2 * step + flip)
            lags = pl.ds(pl.multiple_of(piece * piece_lags, LANES), piece_lags)
            out_ref[step] = whole_ref[:, lags].astype(out_ref.dtype)


def place_kernel(piece_ref, *refs):
    *step_refs, out_ref, held_ref = refs
    for step, ref in enumerate(reversed(step_refs)):
        held_ref[2 * step : 2 * step + 2] = ref[...]
    pieces = held_ref.shape[0]
    cell = held_ref.shape[1] // NGRP
    for source in range(pieces):
        block = held_ref[piece_ref[0] ^ source].astype(jnp.float32)
        for group in range(NGRP):
            out_ref[group, source * cell : (source + 1) * cell, :] = block[group * cell : (group + 1) * cell]


def pair_order(pair_blocks, live_pairs, stack_group, parts, part_blocks, unit_pairs, spare_units):
    owners, slots, _ = pair_blocks.shape
    total = owners * slots
    places = (-(-total // unit_pairs) + NGRP + spare_units) * unit_pairs
    group_index = jnp.arange(NGRP, dtype=jnp.int32)
    live = jnp.arange(slots, dtype=jnp.int32)[None, :] < live_pairs[:, None]
    member = (stack_group[:, :, None] == group_index) & live[:, :, None]
    member = member.reshape(total, NGRP).astype(jnp.int32)
    members = jnp.sum(member, axis=0)
    filled = (members + unit_pairs - 1) // unit_pairs * unit_pairs
    ends = jnp.cumsum(filled)
    rank = jnp.cumsum(member, axis=0) - 1
    place = jnp.sum(member * (rank + (ends - filled)[None, :] + 1), axis=1) - 1
    here = jnp.arange(places, dtype=jnp.int32)
    match = here[:, None] == place[None, :]
    me = lax.axis_index("pair")
    blocks = pair_blocks.reshape(total, 2).T
    held = (lax.rem(blocks, parts) ^ me) * part_blocks + blocks // parts
    empty = parts * part_blocks
    taken = jnp.sum(jnp.where(match[None], held[:, None, :] - empty, 0), axis=2) + empty
    unit_start = jnp.arange(places // unit_pairs, dtype=jnp.int32) * unit_pairs
    unit_group = jnp.minimum(jnp.sum((unit_start[:, None] >= ends[None, :]).astype(jnp.int32), axis=1), NGRP - 1)
    norm = 1.0 / jnp.sqrt(members.astype(jnp.float32))
    return ends[-1:] // unit_pairs, taken, unit_group, norm


def chunk_cells(own_channels, parts, cores):
    if (own_channels, parts, cores) != (2 * SUB_ROWS, 4, 2):
        return [[1] * own_channels]
    return [[8], [4], [4]]


def shards(spectra, pair_blocks, live_pairs, stack_group):
    parts = lax.axis_size("pair")
    me = lax.axis_index("pair")
    cores = lax.axis_size("lag")
    core = lax.axis_index("lag")
    part_blocks, _, channels, width = spectra.shape
    num_bins = width // 2
    lag_count = 2 * num_bins
    own_channels = channels // (parts * cores)
    chunks = chunk_cells(own_channels, parts, cores)
    unit_pairs = PACK_ROWS // min(chunks[-1])
    pieces = parts * cores
    here = (me * cores + core).reshape(1)
    tile_units = [max(1, rows // chunk_rows(cells, unit_pairs)) for cells, rows in zip(chunks, (256, 128, 128))]

    used, taken, unit_group, norm = pair_order(
        pair_blocks, live_pairs, stack_group, parts, part_blocks, unit_pairs, max(tile_units)
    )

    def stack_call(cells, units, received, done):
        rows = part_blocks * sum(cells)
        if rows % PACK_ROWS:
            received = [jnp.concatenate(received, axis=0)]
        tiles = (used + units - 1) // units
        smem, vmem = pl.BlockSpec(memory_space=pltpu.SMEM), pl.BlockSpec(memory_space=pltpu.VMEM)
        tile_rows = units * chunk_rows(cells, unit_pairs)
        in_specs = [smem] * 4 + [vmem] * (len(received) + 1)
        args = [tiles, taken, unit_group, norm, *received, table]
        out_shape = jax.ShapeDtypeStruct((NGRP, sum(cells), lag_count), jnp.float32)
        scratch = [pltpu.VMEM((parts * part_blocks + 1, SUB_ROWS, width), jnp.float32) for _ in cells]
        scratch += [
            pltpu.VMEM((tile_rows, width), jnp.bfloat16),
            pltpu.VMEM((lag_count // CLASSES // LANES, CLASSES, tile_rows, 2 * LANES), jnp.float32),
            pltpu.VMEM((3, NGRP, len(cells), SUB_ROWS, lag_count), jnp.float32),
        ]
        out_specs = vmem
        if done:
            in_specs += [smem] + [vmem] * len(done)
            args += [here, *done]
            piece = jax.ShapeDtypeStruct((parts, NGRP * own_channels, lag_count // pieces), jnp.bfloat16)
            out_shape, out_specs = [piece, piece], [vmem, vmem]
            scratch.append(pltpu.VMEM((NGRP * own_channels, lag_count), jnp.float32))
        return pl.pallas_call(
            functools.partial(stack_kernel, len(received), cells, unit_pairs, units, len(done)),
            out_shape=out_shape,
            in_specs=in_specs,
            out_specs=out_specs,
            scratch_shapes=scratch,
            compiler_params=pltpu.CompilerParams(vmem_limit_bytes=20 * 1024 * 1024),
            name="stack",
        )(*args)

    def move(value, shift):
        return lax.ppermute(value, "pair", [(i, i ^ shift) for i in range(parts)])

    starts = [((me ^ step) * cores + core) * own_channels for step in range(parts)]
    if len(chunks) > 1:
        pieces_of = [[None] * parts for _ in chunks]
        raw = {}
        calls = [[(2, 0)], [(3, 0), (1, 0)], [(0, 0)] + [(step, index) for index in range(1, len(chunks)) for step in range(parts)]]
        for wanted in calls:
            steps = list(dict.fromkeys(step for step, _ in wanted))
            for step in steps:
                if step not in raw:
                    raw[step] = lax.dynamic_slice_in_dim(spectra, starts[step], own_channels, 2)
            flat = pl.pallas_call(
                functools.partial(prepare_kernel, chunks, wanted),
                out_shape=[
                    jax.ShapeDtypeStruct((part_blocks * sum(chunks[index]), width), jnp.bfloat16)
                    for _, index in wanted
                ],
                in_specs=[pl.BlockSpec(memory_space=pltpu.VMEM)] * len(steps),
                out_specs=[pl.BlockSpec(memory_space=pltpu.VMEM)] * len(wanted),
                compiler_params=pltpu.CompilerParams(vmem_limit_bytes=16 * 1024 * 1024),
                name="prepare",
            )(*[raw[step] for step in steps])
            flat = list(flat)
            flat[0], starts = lax.optimization_barrier((flat[0], starts))
            for (step, index), piece in zip(wanted, flat):
                pieces_of[index][step] = piece
    else:
        ordered = whiten(spectra).reshape(part_blocks, channels, 2, num_bins // CLASSES, CLASSES)
        ordered = ordered.swapaxes(3, 4).reshape(part_blocks, channels, width)
        pieces_of = [[]]
        for step in range(parts):
            piece = lax.dynamic_slice_in_dim(ordered, starts[step], own_channels, 1)
            pieces_of[0].append(piece.reshape(part_blocks * own_channels, width))

    received, done = [], []
    for index, (cells, units, chunk) in enumerate(zip(chunks, tile_units, pieces_of)):
        if index == 1:
            chunk[1:], received[0][2] = lax.optimization_barrier((chunk[1:], received[0][2]))
        if index > 1:
            chunk[1:], done[index - 2] = lax.optimization_barrier((chunk[1:], done[index - 2]))
        received.append([chunk[0]] + [move(chunk[step], step) for step in range(1, parts)])
        if index == 0:
            if parts > 2:
                used, received[0][2] = lax.optimization_barrier((used, received[0][2]))
            table = lag_table(used, lag_count, num_bins)
        if len(chunks) == 1:
            return lax.all_to_all(stack_call(cells, units, received[0], []), ("pair", "lag"), 2, 1, tiled=True)
        if index < len(chunks) - 1:
            done.append(stack_call(cells, units, received[index], []))

    near, far = stack_call(chunks[-1], tile_units[-1], received[-1], done)
    other = lax.ppermute(far, "lag", [(i, i ^ 1) for i in range(cores)])
    both = jnp.stack([near, other], 1)
    arrived = [both[0]] + [move(both[step], step) for step in range(1, parts)]
    return pl.pallas_call(
        place_kernel,
        out_shape=jax.ShapeDtypeStruct((NGRP, channels, lag_count // pieces), jnp.float32),
        in_specs=[pl.BlockSpec(memory_space=pltpu.SMEM)] + [pl.BlockSpec(memory_space=pltpu.VMEM)] * parts,
        out_specs=pl.BlockSpec(memory_space=pltpu.VMEM),
        scratch_shapes=[pltpu.VMEM((pieces, NGRP * own_channels, lag_count // pieces), jnp.bfloat16)],
        compiler_params=pltpu.CompilerParams(vmem_limit_bytes=8 * 1024 * 1024),
        name="place",
    )(here, *reversed(arrived))


def solution(mesh):
    return jax.shard_map(
        shards,
        mesh=mesh,
        in_specs=(P("win", "pair", "stk", None), P("win", None, None), P("win"), P("win", None)),
        out_specs=P("win", "stk", ("pair", "lag")),
        check_vma=False,
    )
```

```python
import functools
import math

import jax
import jax.numpy as jnp
from jax import lax
from jax.experimental import pallas as pl
from jax.experimental.pallas import tpu as pltpu
from jax.sharding import PartitionSpec as P

NGRP = 4
HW = 15

AMP_FLOOR = 0.5
EPSILON = 1e-06
TILE_ROWS = 256
PACK_ROWS = 16
SUB_ROWS = 8
LANES = 128
CLASSES = 4


def turn(steps, period):
    quarter = period // 4
    quadrant = (steps + quarter // 2) // quarter
    angle = (steps - quadrant * quarter).astype(jnp.float32) * (2.0 * math.pi / period)
    square = angle * angle
    cosine = 1.0 + square * (-1 / 2 + square * (1 / 24 + square * (-1 / 720 + square * (1 / 40320))))
    sine = angle * (1.0 + square * (-1 / 6 + square * (1 / 120 + square * (-1 / 5040 + square * (1 / 362880)))))
    odd = (quadrant & 1) == 1
    cosine, sine = jnp.where(odd, sine, cosine), jnp.where(odd, cosine, sine)
    cosine = jnp.where(((quadrant + 1) & 2) == 2, -cosine, cosine)
    sine = jnp.where((quadrant & 2) == 2, -sine, sine)
    return cosine, sine


def table_kernel(used_ref, out_ref):
    width, columns = out_ref.shape
    num_bins = width // 2
    period = 2 * num_bins
    scale = math.sqrt(2.0 / num_bins)
    class_bins = num_bins // CLASSES
    rows = lax.broadcasted_iota(jnp.int32, (class_bins, LANES), 0)
    lanes = lax.broadcasted_iota(jnp.int32, (class_bins, LANES), 1)
    for index in range(CLASSES):
        real_rows = slice(2 * index * class_bins, (2 * index + 1) * class_bins)
        imag_rows = slice((2 * index + 1) * class_bins, (2 * index + 2) * class_bins)
        for tile in range(columns // (2 * LANES)):
            lags = lanes + (tile * LANES + num_bins)
            cosine, sine = turn((rows * CLASSES + index) * lags & (period - 1), period)
            cosine, sine = cosine * scale, sine * scale
            direct = slice(2 * tile * LANES, (2 * tile + 1) * LANES)
            quad = slice((2 * tile + 1) * LANES, (2 * tile + 2) * LANES)
            out_ref[real_rows, direct] = cosine.astype(jnp.bfloat16)
            out_ref[imag_rows, direct] = (-sine).astype(jnp.bfloat16)
            out_ref[real_rows, quad] = sine.astype(jnp.bfloat16)
            out_ref[imag_rows, quad] = cosine.astype(jnp.bfloat16)


def lag_table(used, lag_count, num_bins):
    return pl.pallas_call(
        table_kernel,
        out_shape=jax.ShapeDtypeStruct((2 * num_bins, 2 * lag_count // CLASSES), jnp.bfloat16),
        in_specs=[pl.BlockSpec(memory_space=pltpu.SMEM)],
        out_specs=pl.BlockSpec(memory_space=pltpu.VMEM),
        compiler_params=pltpu.CompilerParams(vmem_limit_bytes=6 * 1024 * 1024),
        name="table",
    )(used)


def whiten(values):
    values = values.astype(jnp.float32)
    power = jnp.sum(values * values, axis=-1, keepdims=True) * (2.0 / values.shape[-1])
    return (values * lax.rsqrt(power + EPSILON)).astype(jnp.bfloat16)


def prepare_kernel(cells_of, *refs):
    in_refs = refs[: len(cells_of)]
    out_refs = list(refs[len(cells_of) :])
    rows, width = in_refs[0].shape
    num_bins = width // 2
    class_bins = num_bins // CLASSES
    source = lax.broadcasted_iota(jnp.int32, (num_bins, num_bins), 0)
    target = lax.broadcasted_iota(jnp.int32, (num_bins, num_bins), 1)
    moved = (target & (class_bins - 1)) * CLASSES + target // class_bins
    shuffle = jnp.where(source == moved, 1.0, 0.0).astype(jnp.bfloat16)
    for in_ref, cells in zip(in_refs, cells_of):
        white = whiten(in_ref[...])
        cell_refs = [out_refs.pop(0) for _ in cells]
        for start in (0, num_bins):
            half = jnp.dot(white[:, start : start + num_bins], shuffle, preferred_element_type=jnp.float32)
            bins = slice(start, start + num_bins)
            if len(cells) == 1:
                cell_refs[0][:, bins] = half.astype(jnp.bfloat16)
                continue
            half = half.reshape(rows // SUB_ROWS, SUB_ROWS, num_bins)
            offset = 0
            for cell, out_ref in zip(cells, cell_refs):
                blocks = PACK_ROWS // cell
                for first in range(0, rows // SUB_ROWS, blocks):
                    pack = [half[first + k, offset : offset + cell] for k in range(blocks)]
                    out_ref[first * cell : first * cell + PACK_ROWS, bins] = jnp.concatenate(pack, axis=0).astype(
                        jnp.bfloat16
                    )
                offset += cell


def prepare(pieces, cells_of):
    rows, width = pieces[0].shape
    vmem = pl.BlockSpec(memory_space=pltpu.VMEM)
    shapes = [
        jax.ShapeDtypeStruct((rows // SUB_ROWS * cell, width), jnp.bfloat16) for cells in cells_of for cell in cells
    ]
    return list(
        pl.pallas_call(
            functools.partial(prepare_kernel, cells_of),
            out_shape=shapes,
            in_specs=[vmem] * len(pieces),
            out_specs=[vmem] * len(shapes),
            compiler_params=pltpu.CompilerParams(vmem_limit_bytes=16 * 1024 * 1024),
            name="prepare",
        )(*pieces)
    )


def window_sum(values):
    rows, lags = values.shape
    edge = jnp.zeros((rows, 128), jnp.float32)
    one = jnp.concatenate([edge, values, edge], axis=1)
    width = one.shape[1]
    two = one + pltpu.roll(one, 1, 1)
    four = two + pltpu.roll(two, 2, 1)
    eight = four + pltpu.roll(four, 4, 1)
    back = eight + pltpu.roll(eight, 8, 1)
    ahead = eight + pltpu.roll(four, 8, 1) + pltpu.roll(two, 12, 1) + pltpu.roll(one, 14, 1)
    return (back + pltpu.roll(ahead, width - HW, 1))[:, 128 : 128 + lags]


def chunk_rows(cells, unit_pairs):
    return unit_pairs * sum(cells)


def quarter_turns(direct, quad):
    even_d, even_q = direct[0] + direct[2], quad[0] + quad[2]
    odd_d, odd_q = direct[1] + direct[3], quad[1] + quad[3]
    even_e, even_r = direct[0] - direct[2], quad[0] - quad[2]
    odd_e, odd_r = direct[1] - direct[3], quad[1] - quad[3]
    return (
        [even_d + odd_d, even_e - odd_r, even_d - odd_d, even_e + odd_r],
        [even_q + odd_q, even_r + odd_e, even_q - odd_q, even_r - odd_e],
    )


def phase_terms(direct, quad):
    inverse = jnp.minimum(lax.rsqrt(direct * direct + quad * quad), 1.0 / AMP_FLOOR)
    return [direct, direct * inverse, quad * inverse]


def stack_kernel(num_parts, cells, unit_pairs, tile_units, num_done, tiles_ref, place_ref, groups_ref, norm_ref, *refs):
    refs = list(refs)
    part_refs = [refs.pop(0) for _ in range(num_parts)]
    table_ref = refs.pop(0)
    if num_done:
        piece_ref = refs.pop(0)
        done_refs = [refs.pop(0) for _ in range(num_done)]
        near_ref, far_ref = refs.pop(0), refs.pop(0)
    else:
        out_ref = refs.pop(0)
    white_refs = [refs.pop(0) for _ in cells]
    cross_ref, lag_ref, sums_ref = refs[:3]
    part_rows, width = part_refs[0].shape
    num_bins = width // 2
    class_bins = num_bins // CLASSES
    quarter = width // CLASSES
    unit_rows = chunk_rows(cells, unit_pairs)
    part_blocks = part_rows // sum(cells)

    for part, ref in enumerate(part_refs):
        start = 0
        for cell, white_ref in zip(cells, white_refs):
            rows = part_blocks * cell
            copies = SUB_ROWS // cell
            white = ref[start : start + rows, :].astype(jnp.float32).reshape(rows // SUB_ROWS, SUB_ROWS, width)
            start += rows
            if copies == 1:
                white_ref[part * part_blocks : (part + 1) * part_blocks] = white
            else:
                for sub in range(rows // SUB_ROWS):
                    for copy in range(copies):
                        block = white[sub, copy * cell : (copy + 1) * cell]
                        white_ref[part * part_blocks + sub * copies + copy] = jnp.concatenate([block] * copies, axis=0)
    for white_ref in white_refs:
        white_ref[white_ref.shape[0] - 1] = jnp.zeros((SUB_ROWS, width), jnp.float32)
    sums_ref[...] = jnp.zeros_like(sums_ref)
    sub_row = lax.broadcasted_iota(jnp.int32, (SUB_ROWS, width), 0)

    def pick(white_ref, cell, side, place):
        rows = white_ref[place_ref[side, place]]
        for copy in range(1, SUB_ROWS // cell):
            other = white_ref[place_ref[side, place + copy]]
            rows = jnp.where(sub_row < copy * cell, rows, other)
        return rows

    subs = []
    for index, cell in enumerate(cells):
        subs += [(index, cell, pair) for pair in range(0, unit_pairs, SUB_ROWS // cell)]

    def tile_step(tile, carry):
        for unit in range(tile_units):
            for pack in range(0, len(subs), PACK_ROWS // SUB_ROWS):
                real_parts, imag_parts = [], []
                for index, cell, pair in subs[pack : pack + PACK_ROWS // SUB_ROWS]:
                    place = (tile * tile_units + unit) * unit_pairs + pair
                    first = pick(white_refs[index], cell, 0, place)
                    second = pick(white_refs[index], cell, 1, place)
                    real_a, imag_a = first[:, :num_bins], first[:, num_bins:]
                    real_b, imag_b = second[:, :num_bins], second[:, num_bins:]
                    real_parts.append(real_a * real_b + imag_a * imag_b)
                    imag_parts.append(imag_a * real_b - real_a * imag_b)
                start = unit * unit_rows + pack * SUB_ROWS
                own = slice(start, start + PACK_ROWS)
                real_part = jnp.concatenate(real_parts, axis=0).astype(jnp.bfloat16)
                imag_part = jnp.concatenate(imag_parts, axis=0).astype(jnp.bfloat16)
                for index in range(CLASSES):
                    bins = slice(index * class_bins, (index + 1) * class_bins)
                    middle = (2 * index + 1) * class_bins
                    cross_ref[own, middle - class_bins : middle] = real_part[:, bins]
                    cross_ref[own, middle : middle + class_bins] = imag_part[:, bins]
        for lag in range(quarter // LANES):
            for index in range(CLASSES):
                rows = slice(2 * index * class_bins, 2 * (index + 1) * class_bins)
                lag_ref[lag, index] = jnp.dot(
                    cross_ref[:, rows],
                    table_ref[rows, 2 * lag * LANES : 2 * (lag + 1) * LANES],
                    preferred_element_type=jnp.float32,
                )
        for lag in range(quarter // LANES):
            for unit in range(tile_units):
                group = groups_ref[tile * tile_units + unit]
                totals = [None] * len(cells)
                for sub, (index, _, _) in enumerate(subs):
                    start = unit * unit_rows + sub * SUB_ROWS
                    own = slice(start, start + SUB_ROWS)
                    direct = [lag_ref[lag, k, own, :LANES] for k in range(CLASSES)]
                    quad = [lag_ref[lag, k, own, LANES:] for k in range(CLASSES)]
                    terms = [phase_terms(d, q) for d, q in zip(*quarter_turns(direct, quad))]
                    if totals[index] is None:
                        totals[index] = terms
                    else:
                        totals[index] = [
                            [one + two for one, two in zip(old, new)] for old, new in zip(totals[index], terms)
                        ]
                for index, total in enumerate(totals):
                    for turn_index, kinds in enumerate(total):
                        lags = slice(turn_index * quarter + lag * LANES, turn_index * quarter + (lag + 1) * LANES)
                        for kind, value in enumerate(kinds):
                            sums_ref[kind, group, index, :, lags] += value
        return carry

    lax.fori_loop(0, tiles_ref[0], tile_step, 0)

    linear, coherence = [], []
    for group in range(NGRP):
        scale = norm_ref[group]
        for index, cell in enumerate(cells):
            folded = []
            for kind in range(3):
                whole = sums_ref[kind, group, index]
                total = whole[:cell]
                for start in range(cell, SUB_ROWS, cell):
                    total = total + whole[start : start + cell]
                folded.append(total)
            linear.append(folded[0] * scale)
            coherence.append(jnp.sqrt(folded[1] * folded[1] + folded[2] * folded[2]) * scale)
    smoothed = window_sum(jnp.concatenate(coherence, axis=0)) * (1.0 / (2 * HW + 1))
    stacks = jnp.concatenate(linear, axis=0) * smoothed * smoothed
    channels = sum(cells)
    if not num_done:
        for group in range(NGRP):
            out_ref[group] = stacks[group * channels : (group + 1) * channels]
        return
    whole_ref = refs[3]
    for group in range(NGRP):
        rows = [ref[group] for ref in done_refs] + [stacks[group * channels : (group + 1) * channels]]
        rows = jnp.concatenate(rows, axis=0)
        whole_ref[group * rows.shape[0] : (group + 1) * rows.shape[0], :] = rows
    parts, _, piece_lags = near_ref.shape
    for step in range(parts):
        for flip, out_ref in enumerate((near_ref, far_ref)):
            piece = piece_ref[0] ^ (2 * step + flip)
            lags = pl.ds(pl.multiple_of(piece * piece_lags, LANES), piece_lags)
            out_ref[step] = whole_ref[:, lags].astype(out_ref.dtype)


def place_kernel(piece_ref, *refs):
    *step_refs, out_ref, held_ref = refs
    for step, ref in enumerate(reversed(step_refs)):
        held_ref[2 * step : 2 * step + 2] = ref[...]
    pieces = held_ref.shape[0]
    cell = held_ref.shape[1] // NGRP
    for source in range(pieces):
        block = held_ref[piece_ref[0] ^ source].astype(jnp.float32)
        for group in range(NGRP):
            out_ref[group, source * cell : (source + 1) * cell, :] = block[group * cell : (group + 1) * cell]


def pair_order(pair_blocks, live_pairs, stack_group, parts, part_blocks, unit_pairs, spare_units):
    owners, slots, _ = pair_blocks.shape
    total = owners * slots
    places = (-(-total // unit_pairs) + NGRP + spare_units) * unit_pairs
    group_index = jnp.arange(NGRP, dtype=jnp.int32)
    live = jnp.arange(slots, dtype=jnp.int32)[None, :] < live_pairs[:, None]
    member = (stack_group[:, :, None] == group_index) & live[:, :, None]
    member = member.reshape(total, NGRP).astype(jnp.int32)
    members = jnp.sum(member, axis=0)
    filled = (members + unit_pairs - 1) // unit_pairs * unit_pairs
    ends = jnp.cumsum(filled)
    rank = jnp.cumsum(member, axis=0) - 1
    place = jnp.sum(member * (rank + (ends - filled)[None, :] + 1), axis=1) - 1
    here = jnp.arange(places, dtype=jnp.int32)
    match = here[:, None] == place[None, :]
    me = lax.axis_index("pair")
    blocks = pair_blocks.reshape(total, 2).T
    held = (lax.rem(blocks, parts) ^ me) * part_blocks + blocks // parts
    empty = parts * part_blocks
    taken = jnp.sum(jnp.where(match[None], held[:, None, :] - empty, 0), axis=2) + empty
    unit_start = jnp.arange(places // unit_pairs, dtype=jnp.int32) * unit_pairs
    unit_group = jnp.minimum(jnp.sum((unit_start[:, None] >= ends[None, :]).astype(jnp.int32), axis=1), NGRP - 1)
    norm = 1.0 / jnp.sqrt(members.astype(jnp.float32))
    return ends[-1:] // unit_pairs, taken, unit_group, norm


def chunk_cells(own_channels, parts, cores):
    if (own_channels, parts, cores) != (2 * SUB_ROWS, 4, 2):
        return [[1] * own_channels]
    return [[8], [4], [4]]


def shards(spectra, pair_blocks, live_pairs, stack_group):
    parts = lax.axis_size("pair")
    me = lax.axis_index("pair")
    cores = lax.axis_size("lag")
    core = lax.axis_index("lag")
    part_blocks, _, channels, width = spectra.shape
    num_bins = width // 2
    lag_count = 2 * num_bins
    own_channels = channels // (parts * cores)
    chunks = chunk_cells(own_channels, parts, cores)
    unit_pairs = PACK_ROWS // min(chunks[-1])
    pieces = parts * cores
    here = (me * cores + core).reshape(1)
    tile_units = [max(1, rows // chunk_rows(cells, unit_pairs)) for cells, rows in zip(chunks, (256, 128, 128))]

    used, taken, unit_group, norm = pair_order(
        pair_blocks, live_pairs, stack_group, parts, part_blocks, unit_pairs, max(tile_units)
    )

    def stack_call(cells, units, received, done):
        rows = part_blocks * sum(cells)
        if rows % PACK_ROWS:
            received = [jnp.concatenate(received, axis=0)]
        tiles = (used + units - 1) // units
        smem, vmem = pl.BlockSpec(memory_space=pltpu.SMEM), pl.BlockSpec(memory_space=pltpu.VMEM)
        tile_rows = units * chunk_rows(cells, unit_pairs)
        in_specs = [smem] * 4 + [vmem] * (len(received) + 1)
        args = [tiles, taken, unit_group, norm, *received, table]
        out_shape = jax.ShapeDtypeStruct((NGRP, sum(cells), lag_count), jnp.float32)
        scratch = [pltpu.VMEM((parts * part_blocks + 1, SUB_ROWS, width), jnp.float32) for _ in cells]
        scratch += [
            pltpu.VMEM((tile_rows, width), jnp.bfloat16),
            pltpu.VMEM((lag_count // CLASSES // LANES, CLASSES, tile_rows, 2 * LANES), jnp.float32),
            pltpu.VMEM((3, NGRP, len(cells), SUB_ROWS, lag_count), jnp.float32),
        ]
        out_specs = vmem
        if done:
            in_specs += [smem] + [vmem] * len(done)
            args += [here, *done]
            piece = jax.ShapeDtypeStruct((parts, NGRP * own_channels, lag_count // pieces), jnp.bfloat16)
            out_shape, out_specs = [piece, piece], [vmem, vmem]
            scratch.append(pltpu.VMEM((NGRP * own_channels, lag_count), jnp.float32))
        return pl.pallas_call(
            functools.partial(stack_kernel, len(received), cells, unit_pairs, units, len(done)),
            out_shape=out_shape,
            in_specs=in_specs,
            out_specs=out_specs,
            scratch_shapes=scratch,
            compiler_params=pltpu.CompilerParams(vmem_limit_bytes=20 * 1024 * 1024),
            name="stack",
        )(*args)

    def move(value, shift):
        return lax.ppermute(value, "pair", [(i, i ^ shift) for i in range(parts)])

    starts = [((me ^ step) * cores + core) * own_channels for step in range(parts)]
    if len(chunks) > 1:
        def raw(step, half):
            start = starts[step] + half * SUB_ROWS
            piece = lax.dynamic_slice_in_dim(spectra, start, SUB_ROWS, 2)
            return piece.reshape(part_blocks * SUB_ROWS, width)

        pieces_of = [[None] * parts for _ in chunks]
        pieces_of[0][2] = raw(2, 0)
        pieces_of[0][2], starts = lax.optimization_barrier((pieces_of[0][2], starts))
        flat = prepare([raw(3, 0), raw(1, 0)], [[SUB_ROWS]] * 2)
        flat, starts = lax.optimization_barrier((flat, starts))
        pieces_of[0][3], pieces_of[0][1] = flat
        later = [cell for cells in chunks[1:] for cell in cells]
        flat = prepare([raw(0, 0)] + [raw(step, 1) for step in range(parts)], [[SUB_ROWS]] + [later] * parts)
        pieces_of[0][0] = flat.pop(0)
        for step in range(parts):
            for index in range(1, len(chunks)):
                pieces_of[index][step] = flat.pop(0)
    else:
        ordered = whiten(spectra).reshape(part_blocks, channels, 2, num_bins // CLASSES, CLASSES)
        ordered = ordered.swapaxes(3, 4).reshape(part_blocks, channels, width)
        pieces_of = [[]]
        for step in range(parts):
            piece = lax.dynamic_slice_in_dim(ordered, starts[step], own_channels, 1)
            pieces_of[0].append(piece.reshape(part_blocks * own_channels, width))

    received, done = [], []
    for index, (cells, units, chunk) in enumerate(zip(chunks, tile_units, pieces_of)):
        if index == 1:
            chunk[1:], first_arrived = lax.optimization_barrier((chunk[1:], first_arrived))
            chunk[1], table, received[0][2] = lax.optimization_barrier((chunk[1], table, received[0][2]))
        if index > 1:
            chunk[1:], received[0][3] = lax.optimization_barrier((chunk[1:], received[0][3]))
        got = [chunk[0]] + [None] * (parts - 1)
        for step in sorted(range(1, parts), reverse=index == 0):
            if index == 0 and step == 1 and len(chunks) > 1:
                chunk[1], pieces_of[1][0] = lax.optimization_barrier((chunk[1], pieces_of[1][0]))
            got[step] = move(chunk[step], step)
        received.append(got)
        if index == 0:
            if parts > 2:
                used, received[0][2] = lax.optimization_barrier((used, received[0][2]))
                first_arrived = received[0][2]
            table = lag_table(used, lag_count, num_bins)
            if len(chunks) > 1:
                received[0][2] = prepare([received[0][2]], [[SUB_ROWS]])[0]
        if len(chunks) == 1:
            return lax.all_to_all(stack_call(cells, units, received[0], []), ("pair", "lag"), 2, 1, tiled=True)
        if index < len(chunks) - 1:
            done.append(stack_call(cells, units, received[index], []))

    near, far = stack_call(chunks[-1], tile_units[-1], received[-1], done)
    other = lax.ppermute(far, "lag", [(i, i ^ 1) for i in range(cores)])
    both = jnp.stack([near, other], 1)
    arrived = [both[0]] + [move(both[step], step) for step in range(1, parts)]
    return pl.pallas_call(
        place_kernel,
        out_shape=jax.ShapeDtypeStruct((NGRP, channels, lag_count // pieces), jnp.float32),
        in_specs=[pl.BlockSpec(memory_space=pltpu.SMEM)] + [pl.BlockSpec(memory_space=pltpu.VMEM)] * parts,
        out_specs=pl.BlockSpec(memory_space=pltpu.VMEM),
        scratch_shapes=[pltpu.VMEM((pieces, NGRP * own_channels, lag_count // pieces), jnp.bfloat16)],
        compiler_params=pltpu.CompilerParams(vmem_limit_bytes=8 * 1024 * 1024),
        name="place",
    )(here, *reversed(arrived))


def solution(mesh):
    return jax.shard_map(
        shards,
        mesh=mesh,
        in_specs=(P("win", "pair", "stk", None), P("win", None, None), P("win"), P("win", None)),
        out_specs=P("win", "stk", ("pair", "lag")),
        check_vma=False,
    )
```

```python
import functools
import math

import jax
import jax.numpy as jnp
from jax import lax
from jax.experimental import pallas as pl
from jax.experimental.pallas import tpu as pltpu
from jax.sharding import PartitionSpec as P

NGRP = 4
HW = 15

AMP_FLOOR = 0.5
EPSILON = 1e-06
TILE_ROWS = 256
PACK_ROWS = 16
SUB_ROWS = 8
LANES = 128
CLASSES = 4


def turn(steps, period):
    quarter = period // 4
    quadrant = (steps + quarter // 2) // quarter
    angle = (steps - quadrant * quarter).astype(jnp.float32) * (2.0 * math.pi / period)
    square = angle * angle
    cosine = 1.0 + square * (-1 / 2 + square * (1 / 24 + square * (-1 / 720 + square * (1 / 40320))))
    sine = angle * (1.0 + square * (-1 / 6 + square * (1 / 120 + square * (-1 / 5040 + square * (1 / 362880)))))
    odd = (quadrant & 1) == 1
    cosine, sine = jnp.where(odd, sine, cosine), jnp.where(odd, cosine, sine)
    cosine = jnp.where(((quadrant + 1) & 2) == 2, -cosine, cosine)
    sine = jnp.where((quadrant & 2) == 2, -sine, sine)
    return cosine, sine


def table_kernel(used_ref, out_ref):
    width, columns = out_ref.shape
    num_bins = width // 2
    period = 2 * num_bins
    scale = math.sqrt(2.0 / num_bins)
    class_bins = num_bins // CLASSES
    rows = lax.broadcasted_iota(jnp.int32, (class_bins, LANES), 0)
    lanes = lax.broadcasted_iota(jnp.int32, (class_bins, LANES), 1)
    for index in range(CLASSES):
        real_rows = slice(2 * index * class_bins, (2 * index + 1) * class_bins)
        imag_rows = slice((2 * index + 1) * class_bins, (2 * index + 2) * class_bins)
        for tile in range(columns // (2 * LANES)):
            lags = lanes + (tile * LANES + num_bins)
            cosine, sine = turn((rows * CLASSES + index) * lags & (period - 1), period)
            cosine, sine = cosine * scale, sine * scale
            direct = slice(2 * tile * LANES, (2 * tile + 1) * LANES)
            quad = slice((2 * tile + 1) * LANES, (2 * tile + 2) * LANES)
            out_ref[real_rows, direct] = cosine.astype(jnp.bfloat16)
            out_ref[imag_rows, direct] = (-sine).astype(jnp.bfloat16)
            out_ref[real_rows, quad] = sine.astype(jnp.bfloat16)
            out_ref[imag_rows, quad] = cosine.astype(jnp.bfloat16)


def lag_table(used, lag_count, num_bins):
    return pl.pallas_call(
        table_kernel,
        out_shape=jax.ShapeDtypeStruct((2 * num_bins, 2 * lag_count // CLASSES), jnp.bfloat16),
        in_specs=[pl.BlockSpec(memory_space=pltpu.SMEM)],
        out_specs=pl.BlockSpec(memory_space=pltpu.VMEM),
        compiler_params=pltpu.CompilerParams(vmem_limit_bytes=6 * 1024 * 1024),
        name="table",
    )(used)


def whiten(values):
    values = values.astype(jnp.float32)
    power = jnp.sum(values * values, axis=-1, keepdims=True) * (2.0 / values.shape[-1])
    return (values * lax.rsqrt(power + EPSILON)).astype(jnp.bfloat16)


def prepare_kernel(cells_of, *refs):
    in_refs = refs[: len(cells_of)]
    out_refs = list(refs[len(cells_of) :])
    rows, width = in_refs[0].shape
    num_bins = width // 2
    class_bins = num_bins // CLASSES
    source = lax.broadcasted_iota(jnp.int32, (num_bins, num_bins), 0)
    target = lax.broadcasted_iota(jnp.int32, (num_bins, num_bins), 1)
    moved = (target & (class_bins - 1)) * CLASSES + target // class_bins
    shuffle = jnp.where(source == moved, 1.0, 0.0).astype(jnp.bfloat16)
    for in_ref, cells in zip(in_refs, cells_of):
        white = whiten(in_ref[...])
        cell_refs = [out_refs.pop(0) for _ in cells]
        for start in (0, num_bins):
            half = jnp.dot(white[:, start : start + num_bins], shuffle, preferred_element_type=jnp.float32)
            bins = slice(start, start + num_bins)
            if len(cells) == 1:
                cell_refs[0][:, bins] = half.astype(jnp.bfloat16)
                continue
            half = half.reshape(rows // SUB_ROWS, SUB_ROWS, num_bins)
            offset = 0
            for cell, out_ref in zip(cells, cell_refs):
                blocks = PACK_ROWS // cell
                for first in range(0, rows // SUB_ROWS, blocks):
                    pack = [half[first + k, offset : offset + cell] for k in range(blocks)]
                    out_ref[first * cell : first * cell + PACK_ROWS, bins] = jnp.concatenate(pack, axis=0).astype(
                        jnp.bfloat16
                    )
                offset += cell


def prepare(pieces, cells_of):
    rows, width = pieces[0].shape
    vmem = pl.BlockSpec(memory_space=pltpu.VMEM)
    shapes = [
        jax.ShapeDtypeStruct((rows // SUB_ROWS * cell, width), jnp.bfloat16) for cells in cells_of for cell in cells
    ]
    return list(
        pl.pallas_call(
            functools.partial(prepare_kernel, cells_of),
            out_shape=shapes,
            in_specs=[vmem] * len(pieces),
            out_specs=[vmem] * len(shapes),
            compiler_params=pltpu.CompilerParams(vmem_limit_bytes=16 * 1024 * 1024),
            name="prepare",
        )(*pieces)
    )


def window_sum(values):
    rows, lags = values.shape
    edge = jnp.zeros((rows, 128), jnp.float32)
    one = jnp.concatenate([edge, values, edge], axis=1)
    width = one.shape[1]
    two = one + pltpu.roll(one, 1, 1)
    four = two + pltpu.roll(two, 2, 1)
    eight = four + pltpu.roll(four, 4, 1)
    back = eight + pltpu.roll(eight, 8, 1)
    ahead = eight + pltpu.roll(four, 8, 1) + pltpu.roll(two, 12, 1) + pltpu.roll(one, 14, 1)
    return (back + pltpu.roll(ahead, width - HW, 1))[:, 128 : 128 + lags]


def chunk_rows(cells, unit_pairs):
    return unit_pairs * sum(cells)


def quarter_turns(direct, quad):
    even_d, even_q = direct[0] + direct[2], quad[0] + quad[2]
    odd_d, odd_q = direct[1] + direct[3], quad[1] + quad[3]
    even_e, even_r = direct[0] - direct[2], quad[0] - quad[2]
    odd_e, odd_r = direct[1] - direct[3], quad[1] - quad[3]
    return (
        [even_d + odd_d, even_e - odd_r, even_d - odd_d, even_e + odd_r],
        [even_q + odd_q, even_r + odd_e, even_q - odd_q, even_r - odd_e],
    )


def phase_terms(direct, quad):
    inverse = jnp.minimum(lax.rsqrt(direct * direct + quad * quad), 1.0 / AMP_FLOOR)
    return [direct, direct * inverse, quad * inverse]


def stack_kernel(num_parts, cells, unit_pairs, tile_units, num_done, tiles_ref, place_ref, groups_ref, norm_ref, *refs):
    refs = list(refs)
    part_refs = [refs.pop(0) for _ in range(num_parts)]
    table_ref = refs.pop(0)
    if num_done:
        piece_ref = refs.pop(0)
        done_refs = [refs.pop(0) for _ in range(num_done)]
        near_ref, far_ref = refs.pop(0), refs.pop(0)
    else:
        out_ref = refs.pop(0)
    white_refs = [refs.pop(0) for _ in cells]
    cross_ref, lag_ref, sums_ref = refs[:3]
    part_rows, width = part_refs[0].shape
    num_bins = width // 2
    class_bins = num_bins // CLASSES
    quarter = width // CLASSES
    unit_rows = chunk_rows(cells, unit_pairs)
    part_blocks = part_rows // sum(cells)

    for part, ref in enumerate(part_refs):
        start = 0
        for cell, white_ref in zip(cells, white_refs):
            rows = part_blocks * cell
            copies = SUB_ROWS // cell
            white = ref[start : start + rows, :].astype(jnp.float32).reshape(rows // SUB_ROWS, SUB_ROWS, width)
            start += rows
            if copies == 1:
                white_ref[part * part_blocks : (part + 1) * part_blocks] = white
            else:
                for sub in range(rows // SUB_ROWS):
                    for copy in range(copies):
                        block = white[sub, copy * cell : (copy + 1) * cell]
                        white_ref[part * part_blocks + sub * copies + copy] = jnp.concatenate([block] * copies, axis=0)
    for white_ref in white_refs:
        white_ref[white_ref.shape[0] - 1] = jnp.zeros((SUB_ROWS, width), jnp.float32)
    sums_ref[...] = jnp.zeros_like(sums_ref)
    sub_row = lax.broadcasted_iota(jnp.int32, (SUB_ROWS, width), 0)

    def pick(white_ref, cell, side, place):
        rows = white_ref[place_ref[side, place]]
        for copy in range(1, SUB_ROWS // cell):
            other = white_ref[place_ref[side, place + copy]]
            rows = jnp.where(sub_row < copy * cell, rows, other)
        return rows

    subs = []
    for index, cell in enumerate(cells):
        subs += [(index, cell, pair) for pair in range(0, unit_pairs, SUB_ROWS // cell)]

    def tile_step(tile, carry):
        for unit in range(tile_units):
            for pack in range(0, len(subs), PACK_ROWS // SUB_ROWS):
                real_parts, imag_parts = [], []
                for index, cell, pair in subs[pack : pack + PACK_ROWS // SUB_ROWS]:
                    place = (tile * tile_units + unit) * unit_pairs + pair
                    first = pick(white_refs[index], cell, 0, place)
                    second = pick(white_refs[index], cell, 1, place)
                    real_a, imag_a = first[:, :num_bins], first[:, num_bins:]
                    real_b, imag_b = second[:, :num_bins], second[:, num_bins:]
                    real_parts.append(real_a * real_b + imag_a * imag_b)
                    imag_parts.append(imag_a * real_b - real_a * imag_b)
                start = unit * unit_rows + pack * SUB_ROWS
                own = slice(start, start + PACK_ROWS)
                real_part = jnp.concatenate(real_parts, axis=0).astype(jnp.bfloat16)
                imag_part = jnp.concatenate(imag_parts, axis=0).astype(jnp.bfloat16)
                for index in range(CLASSES):
                    bins = slice(index * class_bins, (index + 1) * class_bins)
                    middle = (2 * index + 1) * class_bins
                    cross_ref[own, middle - class_bins : middle] = real_part[:, bins]
                    cross_ref[own, middle : middle + class_bins] = imag_part[:, bins]
        for lag in range(quarter // LANES):
            for index in range(CLASSES):
                rows = slice(2 * index * class_bins, 2 * (index + 1) * class_bins)
                lag_ref[lag, index] = jnp.dot(
                    cross_ref[:, rows],
                    table_ref[rows, 2 * lag * LANES : 2 * (lag + 1) * LANES],
                    preferred_element_type=jnp.float32,
                )
        for lag in range(quarter // LANES):
            for unit in range(tile_units):
                group = groups_ref[tile * tile_units + unit]
                totals = [None] * len(cells)
                for sub, (index, _, _) in enumerate(subs):
                    start = unit * unit_rows + sub * SUB_ROWS
                    own = slice(start, start + SUB_ROWS)
                    direct = [lag_ref[lag, k, own, :LANES] for k in range(CLASSES)]
                    quad = [lag_ref[lag, k, own, LANES:] for k in range(CLASSES)]
                    terms = [phase_terms(d, q) for d, q in zip(*quarter_turns(direct, quad))]
                    if totals[index] is None:
                        totals[index] = terms
                    else:
                        totals[index] = [
                            [one + two for one, two in zip(old, new)] for old, new in zip(totals[index], terms)
                        ]
                for index, total in enumerate(totals):
                    for turn_index, kinds in enumerate(total):
                        lags = slice(turn_index * quarter + lag * LANES, turn_index * quarter + (lag + 1) * LANES)
                        for kind, value in enumerate(kinds):
                            sums_ref[kind, group, index, :, lags] += value
        return carry

    lax.fori_loop(0, tiles_ref[0], tile_step, 0)

    linear, coherence = [], []
    for group in range(NGRP):
        scale = norm_ref[group]
        for index, cell in enumerate(cells):
            folded = []
            for kind in range(3):
                whole = sums_ref[kind, group, index]
                total = whole[:cell]
                for start in range(cell, SUB_ROWS, cell):
                    total = total + whole[start : start + cell]
                folded.append(total)
            linear.append(folded[0] * scale)
            coherence.append(jnp.sqrt(folded[1] * folded[1] + folded[2] * folded[2]) * scale)
    smoothed = window_sum(jnp.concatenate(coherence, axis=0)) * (1.0 / (2 * HW + 1))
    stacks = jnp.concatenate(linear, axis=0) * smoothed * smoothed
    channels = sum(cells)
    if not num_done:
        for group in range(NGRP):
            out_ref[group] = stacks[group * channels : (group + 1) * channels]
        return
    whole_ref = refs[3]
    for group in range(NGRP):
        rows = [ref[group] for ref in done_refs] + [stacks[group * channels : (group + 1) * channels]]
        rows = jnp.concatenate(rows, axis=0)
        whole_ref[group * rows.shape[0] : (group + 1) * rows.shape[0], :] = rows
    parts, _, piece_lags = near_ref.shape
    for step in range(parts):
        for flip, out_ref in enumerate((near_ref, far_ref)):
            piece = piece_ref[0] ^ (2 * step + flip)
            lags = pl.ds(pl.multiple_of(piece * piece_lags, LANES), piece_lags)
            out_ref[step] = whole_ref[:, lags].astype(out_ref.dtype)


def place_kernel(piece_ref, *refs):
    *step_refs, out_ref, held_ref = refs
    for step, ref in enumerate(reversed(step_refs)):
        held_ref[2 * step : 2 * step + 2] = ref[...]
    pieces = held_ref.shape[0]
    cell = held_ref.shape[1] // NGRP
    for source in range(pieces):
        block = held_ref[piece_ref[0] ^ source].astype(jnp.float32)
        for group in range(NGRP):
            out_ref[group, source * cell : (source + 1) * cell, :] = block[group * cell : (group + 1) * cell]


def pair_order(pair_blocks, live_pairs, stack_group, parts, part_blocks, unit_pairs, spare_units):
    owners, slots, _ = pair_blocks.shape
    total = owners * slots
    places = (-(-total // unit_pairs) + NGRP + spare_units) * unit_pairs
    group_index = jnp.arange(NGRP, dtype=jnp.int32)
    live = jnp.arange(slots, dtype=jnp.int32)[None, :] < live_pairs[:, None]
    member = (stack_group[:, :, None] == group_index) & live[:, :, None]
    member = member.reshape(total, NGRP).astype(jnp.int32)
    members = jnp.sum(member, axis=0)
    filled = (members + unit_pairs - 1) // unit_pairs * unit_pairs
    ends = jnp.cumsum(filled)
    rank = jnp.cumsum(member, axis=0) - 1
    place = jnp.sum(member * (rank + (ends - filled)[None, :] + 1), axis=1) - 1
    here = jnp.arange(places, dtype=jnp.int32)
    match = here[:, None] == place[None, :]
    me = lax.axis_index("pair")
    blocks = pair_blocks.reshape(total, 2).T
    held = (lax.rem(blocks, parts) ^ me) * part_blocks + blocks // parts
    empty = parts * part_blocks
    taken = jnp.sum(jnp.where(match[None], held[:, None, :] - empty, 0), axis=2) + empty
    unit_start = jnp.arange(places // unit_pairs, dtype=jnp.int32) * unit_pairs
    unit_group = jnp.minimum(jnp.sum((unit_start[:, None] >= ends[None, :]).astype(jnp.int32), axis=1), NGRP - 1)
    norm = 1.0 / jnp.sqrt(members.astype(jnp.float32))
    return ends[-1:] // unit_pairs, taken, unit_group, norm


def chunk_cells(own_channels, parts, cores):
    if (own_channels, parts, cores) != (2 * SUB_ROWS, 4, 2):
        return [[1] * own_channels]
    return [[8], [4], [4]]


def shards(spectra, pair_blocks, live_pairs, stack_group):
    parts = lax.axis_size("pair")
    me = lax.axis_index("pair")
    cores = lax.axis_size("lag")
    core = lax.axis_index("lag")
    part_blocks, _, channels, width = spectra.shape
    num_bins = width // 2
    lag_count = 2 * num_bins
    own_channels = channels // (parts * cores)
    chunks = chunk_cells(own_channels, parts, cores)
    unit_pairs = PACK_ROWS // min(chunks[-1])
    pieces = parts * cores
    here = (me * cores + core).reshape(1)
    tile_units = [max(1, rows // chunk_rows(cells, unit_pairs)) for cells, rows in zip(chunks, (256, 160, 160))]

    used, taken, unit_group, norm = pair_order(
        pair_blocks, live_pairs, stack_group, parts, part_blocks, unit_pairs, max(tile_units)
    )

    def stack_call(cells, units, received, done):
        rows = part_blocks * sum(cells)
        if rows % PACK_ROWS:
            received = [jnp.concatenate(received, axis=0)]
        tiles = (used + units - 1) // units
        smem, vmem = pl.BlockSpec(memory_space=pltpu.SMEM), pl.BlockSpec(memory_space=pltpu.VMEM)
        tile_rows = units * chunk_rows(cells, unit_pairs)
        in_specs = [smem] * 4 + [vmem] * (len(received) + 1)
        args = [tiles, taken, unit_group, norm, *received, table]
        out_shape = jax.ShapeDtypeStruct((NGRP, sum(cells), lag_count), jnp.float32)
        scratch = [pltpu.VMEM((parts * part_blocks + 1, SUB_ROWS, width), jnp.float32) for _ in cells]
        scratch += [
            pltpu.VMEM((tile_rows, width), jnp.bfloat16),
            pltpu.VMEM((lag_count // CLASSES // LANES, CLASSES, tile_rows, 2 * LANES), jnp.float32),
            pltpu.VMEM((3, NGRP, len(cells), SUB_ROWS, lag_count), jnp.float32),
        ]
        out_specs = vmem
        if done:
            in_specs += [smem] + [vmem] * len(done)
            args += [here, *done]
            piece = jax.ShapeDtypeStruct((parts, NGRP * own_channels, lag_count // pieces), jnp.bfloat16)
            out_shape, out_specs = [piece, piece], [vmem, vmem]
            scratch.append(pltpu.VMEM((NGRP * own_channels, lag_count), jnp.float32))
        return pl.pallas_call(
            functools.partial(stack_kernel, len(received), cells, unit_pairs, units, len(done)),
            out_shape=out_shape,
            in_specs=in_specs,
            out_specs=out_specs,
            scratch_shapes=scratch,
            compiler_params=pltpu.CompilerParams(vmem_limit_bytes=20 * 1024 * 1024),
            name="stack",
        )(*args)

    def move(value, shift):
        return lax.ppermute(value, "pair", [(i, i ^ shift) for i in range(parts)])

    starts = [((me ^ step) * cores + core) * own_channels for step in range(parts)]
    if len(chunks) > 1:
        def raw(step, half):
            start = starts[step] + half * SUB_ROWS
            piece = lax.dynamic_slice_in_dim(spectra, start, SUB_ROWS, 2)
            return piece.reshape(part_blocks * SUB_ROWS, width)

        pieces_of = [[None] * parts for _ in chunks]
        pieces_of[0][2] = raw(2, 0)
        pieces_of[0][2], starts = lax.optimization_barrier((pieces_of[0][2], starts))
        flat = prepare([raw(3, 0), raw(1, 0)], [[SUB_ROWS]] * 2)
        flat, starts = lax.optimization_barrier((flat, starts))
        pieces_of[0][3], pieces_of[0][1] = flat
        later = [cell for cells in chunks[1:] for cell in cells]
        flat = prepare([raw(0, 0)] + [raw(step, 1) for step in range(parts)], [[SUB_ROWS]] + [later] * parts)
        pieces_of[0][0] = flat.pop(0)
        for step in range(parts):
            for index in range(1, len(chunks)):
                pieces_of[index][step] = flat.pop(0)
    else:
        ordered = whiten(spectra).reshape(part_blocks, channels, 2, num_bins // CLASSES, CLASSES)
        ordered = ordered.swapaxes(3, 4).reshape(part_blocks, channels, width)
        pieces_of = [[]]
        for step in range(parts):
            piece = lax.dynamic_slice_in_dim(ordered, starts[step], own_channels, 1)
            pieces_of[0].append(piece.reshape(part_blocks * own_channels, width))

    received, done = [], []
    for index, (cells, units, chunk) in enumerate(zip(chunks, tile_units, pieces_of)):
        if index == 1:
            chunk[1:], first_arrived = lax.optimization_barrier((chunk[1:], first_arrived))
            chunk[1], table, received[0][2] = lax.optimization_barrier((chunk[1], table, received[0][2]))
        if index > 1:
            chunk[1:], received[0][3] = lax.optimization_barrier((chunk[1:], received[0][3]))
        got = [chunk[0]] + [None] * (parts - 1)
        for step in sorted(range(1, parts), reverse=index == 0):
            if index == 0 and step == 1 and len(chunks) > 1:
                chunk[1], pieces_of[1][0] = lax.optimization_barrier((chunk[1], pieces_of[1][0]))
            got[step] = move(chunk[step], step)
        received.append(got)
        if index == 0:
            if parts > 2:
                used, received[0][2] = lax.optimization_barrier((used, received[0][2]))
                first_arrived = received[0][2]
            table = lag_table(used, lag_count, num_bins)
            if len(chunks) > 1:
                received[0][2] = prepare([received[0][2]], [[SUB_ROWS]])[0]
        if len(chunks) == 1:
            return lax.all_to_all(stack_call(cells, units, received[0], []), ("pair", "lag"), 2, 1, tiled=True)
        if index < len(chunks) - 1:
            done.append(stack_call(cells, units, received[index], []))

    near, far = stack_call(chunks[-1], tile_units[-1], received[-1], done)
    other = lax.ppermute(far, "lag", [(i, i ^ 1) for i in range(cores)])
    both = jnp.stack([near, other], 1)
    arrived = [both[0]] + [move(both[step], step) for step in range(1, parts)]
    return pl.pallas_call(
        place_kernel,
        out_shape=jax.ShapeDtypeStruct((NGRP, channels, lag_count // pieces), jnp.float32),
        in_specs=[pl.BlockSpec(memory_space=pltpu.SMEM)] + [pl.BlockSpec(memory_space=pltpu.VMEM)] * parts,
        out_specs=pl.BlockSpec(memory_space=pltpu.VMEM),
        scratch_shapes=[pltpu.VMEM((pieces, NGRP * own_channels, lag_count // pieces), jnp.bfloat16)],
        compiler_params=pltpu.CompilerParams(vmem_limit_bytes=8 * 1024 * 1024),
        name="place",
    )(here, *reversed(arrived))


def solution(mesh):
    return jax.shard_map(
        shards,
        mesh=mesh,
        in_specs=(P("win", "pair", "stk", None), P("win", None, None), P("win"), P("win", None)),
        out_specs=P("win", "stk", ("pair", "lag")),
        check_vma=False,
    )
```
